128 devices in a mesh: gx: 8 (over y, core), yz: 16 (over z, x).
Axes of the slice: x: 4, y: 4, z: 4, core: 2. Of those that a mesh axis runs over, the one named last changes fastest.
Arguments:
- coeffs: bfloat16 [2048, 16, 256], P(('gx', 'yz')), may hold values from -6 to 6
- occupation: float32 [2048], P(('gx', 'yz')), may hold values from 0.5 to 2
- box_offset: int32 [2048, 3], P(('gx', 'yz')), may hold values from 0 to 496, as said below
- live_count: int32 [128], P(('gx', 'yz')), may hold values from 4 to 16, as said below
- synthesis: float32 [16, 16], replicated
- v_ext: float32 [192, 512, 128], P('gx', 'yz'), may hold values from -6 to 6
- core_density: float32 [192, 512, 128], P('gx', 'yz'), may hold values from 0.05 to 1
Outputs:
- hpsi: bfloat16 [2048, 16, 256], P(('gx', 'yz'))
- potential: float32 [192, 512, 128], P('gx', 'yz')
The draws below stay inside these ranges and needn't reach their ends.
Inputs may be any that keep to these rules, and one draw needn't show every extreme that they name: `box_offset`: A function's box begins inside its owner's domain: the first coordinate lies in the owner's 24 planes along gx and the second in its 32 rows along yz; every box lies inside the grid. `live_count`: A device's used slots are its first ones; some device uses all 16.
All inputs are finite; a program needn't handle non-finite values.
Results may differ from the reference program's by a relative error of at most 0.001.
Values sent between devices are 32-bit elements; how exact they have to be, the bound alone decides.
A program may use at most 128 MiB of HBM per device.

```python
import math
import jax
import jax.numpy as jnp
from jax import lax

EDGE = 16
SLOTS = 16
CX = 24
CY = 32
NZ = 128
FUNCS = 2048
NX = 192
NY = 512
N_GX = 8
N_YZ = 16


def draw_box_offset(key, part):
    key = jax.random.fold_in(key, 11)
    rows = jnp.arange(FUNCS, dtype=jnp.int32)
    device = rows // SLOTS
    slab = device // N_YZ
    column = device % N_YZ
    high_x = jnp.where(slab == N_GX - 1, CX - EDGE + 1, CX)
    high_y = jnp.where(column == N_YZ - 1, CY - EDGE + 1, CY)
    first = jax.random.randint(jax.random.fold_in(key, 1), (FUNCS,), 0, high_x)
    second = jax.random.randint(jax.random.fold_in(key, 2), (FUNCS,), 0, high_y)
    third = jax.random.randint(jax.random.fold_in(key, 3), (FUNCS,), 0, NZ - EDGE + 1)
    result = jnp.stack([slab * CX + first, column * CY + second, third], axis=1).astype(jnp.int32)
    result = result.at[0].set(jnp.zeros((3,), jnp.int32))
    corner = jnp.array([NX - EDGE, NY - EDGE, NZ - EDGE], jnp.int32)
    result = result.at[FUNCS - 1].set(corner)
    return result.astype(jnp.int32)


def draw_live_count(key, part):
    key = jax.random.fold_in(key, 23)
    counts = jax.random.randint(jax.random.fold_in(key, 1), (N_GX * N_YZ,), SLOTS // 4, SLOTS + 1)
    chosen = jax.random.randint(jax.random.fold_in(key, 2), (), 0, N_GX * N_YZ)
    counts = counts.at[chosen].set(SLOTS)
    other = (chosen + 1) % (N_GX * N_YZ)
    return counts.at[other].set(SLOTS // 4).astype(jnp.int32)


def draw_synthesis(key, part):
    key = jax.random.fold_in(key, 37)
    rows = jnp.arange(EDGE)[:, None]
    cols = jnp.arange(EDGE)[None, :]
    band = jnp.abs(rows - cols) <= 3
    noise = 0.2 * jax.random.normal(key, (EDGE, EDGE), jnp.float32)
    return jnp.where(rows == cols, 1.0, jnp.where(band, noise, 0.0)).astype(jnp.float32)


def level_of(rng, dims, shards, low, high):
    gain = 1.0
    for dim, blocks in shards:
        heights = jax.random.uniform(jax.random.fold_in(jax.random.fold_in(rng, 6), dim), (blocks,), jnp.float32, low / len(shards), high / len(shards))
        gain = gain * jnp.repeat(jnp.exp(heights), dims[dim] // blocks).reshape((-1,) + (1,) * (len(dims) - 1 - dim))
    return gain


def centred(rng, dims, scale, bound, shards=(), kind=jnp.bfloat16):
    values = scale * jax.random.normal(rng, dims, jnp.float32)
    if shards:
        values = values * level_of(rng, dims, shards, -0.22, 0.18)
    return jnp.clip(values, -bound, bound).astype(kind)


def setup_inputs(seed: int = 0) -> dict:
    arg_keys = jax.random.split(jax.random.key(seed), 8)
    return {
        "coeffs": centred(arg_keys[0], (FUNCS, EDGE, EDGE * EDGE), 1.0, 6.0, ((0, 128),)),
        "occupation": jnp.clip(jnp.exp(math.log(2.0) - 1.3862944 * jax.random.uniform(arg_keys[1], (FUNCS,), jnp.float32) ** level_of(arg_keys[1], (FUNCS,), ((0, 128),), -0.2, 0.2)), 0.5, 2.0),
        "box_offset": draw_box_offset(jax.random.fold_in(arg_keys[7], 71), 0),
        "live_count": draw_live_count(jax.random.fold_in(arg_keys[7], 71), 0),
        "synthesis": draw_synthesis(jax.random.fold_in(arg_keys[7], 71), 0),
        "v_ext": centred(arg_keys[5], (NX, NY, NZ), 1.0, 6.0, ((0, 8), (1, 16)), jnp.float32),
        "core_density": jnp.clip(jnp.exp(math.log(1.0) - 2.9957323 * jax.random.uniform(arg_keys[6], (NX, NY, NZ), jnp.float32) ** level_of(arg_keys[6], (NX, NY, NZ), ((0, 8), (1, 16)), -0.2, 0.2)), 0.05, 1.0),
    }


XC_COEF = -0.9847450218426964


def synthesize(values, synthesis):
    highest = lax.Precision.HIGHEST
    values = jnp.einsum("ai,fijk->fajk", synthesis, values, precision=highest)
    values = jnp.einsum("bj,fajk->fabk", synthesis, values, precision=highest)
    return jnp.einsum("ck,fabk->fabc", synthesis, values, precision=highest)


def analyze(values, synthesis):
    highest = lax.Precision.HIGHEST
    values = jnp.einsum("ai,fabc->fibc", synthesis, values, precision=highest)
    values = jnp.einsum("bj,fibc->fijc", synthesis, values, precision=highest)
    return jnp.einsum("ck,fijc->fijk", synthesis, values, precision=highest)


def reference(coeffs, occupation, box_offset, live_count, synthesis, v_ext, core_density):
    blocks = coeffs.astype(jnp.float32).reshape(FUNCS, EDGE, EDGE, EDGE)
    psi = synthesize(blocks, synthesis)
    slot = jnp.arange(FUNCS, dtype=jnp.int32)
    owner = slot // SLOTS
    live = ((slot % SLOTS) < live_count[owner]).astype(jnp.float32)
    weighted = psi * psi * (occupation * live)[:, None, None, None]
    steps = jnp.arange(EDGE, dtype=jnp.int32)
    start_x = box_offset[:, 0][:, None, None, None] + steps[None, :, None, None]
    start_y = box_offset[:, 1][:, None, None, None] + steps[None, None, :, None]
    start_z = box_offset[:, 2][:, None, None, None] + steps[None, None, None, :]
    flat = ((start_x * NY + start_y) * NZ + start_z).astype(jnp.int32)
    density = core_density.reshape(-1).at[flat.reshape(-1)].add(weighted.reshape(-1))
    density = density.reshape(NX, NY, NZ)
    potential = v_ext + XC_COEF * jnp.cbrt(density)
    values = potential.reshape(-1)[flat]
    applied = analyze(values * psi, synthesis) * live[:, None, None, None]
    hpsi = applied.astype(jnp.bfloat16).reshape(FUNCS, EDGE, EDGE * EDGE)
    return (hpsi, potential)
```

```python
import functools

import jax
import jax.numpy as jnp
from jax import lax
from jax.experimental import pallas as pl
from jax.experimental.pallas import tpu as pltpu
from jax.sharding import PartitionSpec as P

XC_COEF = -0.9847450218426964
EDGE = 16
CUBE = EDGE * EDGE
REACH = EDGE - 1
PAIR = 2
GROUP = 3
F32 = jnp.float32
BF16 = jnp.bfloat16
HIGHEST = lax.Precision.HIGHEST
MESH = pl.DeviceIdType.MESH


def iota(shape, dim):
    return lax.broadcasted_iota(jnp.int32, shape, dim)


def split(value):
    high = value.astype(BF16)
    low = (value - high.astype(F32)).astype(BF16)
    return high, low


def dot(left, right):
    return lax.dot_general(left, right, (((1,), (0,)), ((), ())), preferred_element_type=F32)


def dot_nt(left, right):
    return lax.dot_general(left, right, (((1,), (1,)), ((), ())), preferred_element_type=F32)


def swap_in_blocks(value):
    halves = []
    for half in range(CUBE // 128):
        part = value[:, half * 128 : (half + 1) * 128].reshape(CUBE // 8, 8, 128)
        row, col = iota(part.shape, 1), iota(part.shape, 2)
        for step in (1, 2, 4):
            up = pltpu.roll(pltpu.roll(part, 8 - step, 1), step, 2)
            down = pltpu.roll(pltpu.roll(part, step, 1), 128 - step, 2)
            moved = jnp.where((row & step) != 0, down, up)
            part = jnp.where(((row ^ col) & step) == 0, part, moved)
        part = part.reshape(EDGE, 2, 8, 128)
        first, second = part[:, 0], part[:, 1]
        far = (iota(first.shape, 2) & 8) != 0
        new_first = jnp.where(far, pltpu.roll(second, 8, 2), first)
        new_second = jnp.where(far, second, pltpu.roll(first, 120, 2))
        halves.append(jnp.stack([new_first, new_second], axis=1).reshape(CUBE, 128))
    return jnp.concatenate(halves, axis=1)


def kernel(
    sizes,
    occ_ref, off_ref, live_ref, syn_ref, coef_hbm, vext_hbm, core_hbm,
    hpsi_ref, pot_hbm,
    coef, vext, core, swapped, kron_hi, kron_lo, filt, psi, padded, partial, from_x, from_y, from_c, ext, back,
    in_sems, out_sems, send1, recv1, send2, recv2,
):
    slots, rows_x, rows_y, depth, n_gx, n_yz = sizes
    gx, yz = lax.axis_index("gx"), lax.axis_index("yz")
    wide_y = rows_y + EDGE
    stride = wide_y

    def corner(f):
        x = jnp.clip(off_ref[f, 0] - gx * rows_x, 0, rows_x - 1)
        y = jnp.clip(off_ref[f, 1] - yz * rows_y, 0, rows_y - 1)
        return x, y

    pairs = slots // PAIR

    copy_coef = pltpu.make_async_copy(coef_hbm, coef, in_sems.at[0])
    copy_vext = pltpu.make_async_copy(vext_hbm, vext, in_sems.at[1])
    copy_core = pltpu.make_async_copy(core_hbm, core, in_sems.at[2])
    copy_coef.start()
    copy_core.start()
    copy_vext.start()

    next_x, next_y = lax.rem(gx + 1, n_gx), lax.rem(yz + 1, n_yz)
    last_x, last_y = lax.rem(gx + n_gx - 1, n_gx), lax.rem(yz + n_yz - 1, n_yz)
    barrier = pltpu.get_barrier_semaphore()
    for device in (
        (next_x, yz), (last_x, yz), (gx, next_y), (gx, last_y), (next_x, next_y), (last_x, last_y),
    ):
        pl.semaphore_signal(barrier, inc=1, device_id=device, device_id_type=MESH)

    def clear(slot, carry):
        for plane in range(EDGE + 3):
            padded[slot, pl.ds(stride * plane, rows_y), :] = jnp.zeros((rows_y, depth), F32)
        for plane in (0, EDGE + 1):
            padded[slot, pl.ds(stride * plane + rows_y, EDGE), :] = jnp.zeros((EDGE, depth), F32)
        return carry

    lax.fori_loop(0, slots, clear, 0)

    syn = syn_ref[...]
    lane = iota((EDGE, CUBE), 1)
    row = iota((EDGE, CUBE), 0)
    by_i = lax.dot(syn, (lane % EDGE == row).astype(F32), precision=HIGHEST, preferred_element_type=F32)
    by_j = lax.dot(syn, (lane // EDGE == row).astype(F32), precision=HIGHEST, preferred_element_type=F32)
    for a in range(EDGE):
        high, low = split(by_i[a : a + 1, :] * by_j)
        kron_hi[a * EDGE : (a + 1) * EDGE, :] = high
        kron_lo[a * EDGE : (a + 1) * EDGE, :] = low

    shift = iota((EDGE, depth), 1) - iota((EDGE, depth), 0)
    places = jnp.concatenate([(shift == off_ref[f, 2]).astype(F32) for f in range(slots)], axis=1)
    placed = lax.dot_general(syn, places, (((0,), (0,)), ((), ())), precision=HIGHEST, preferred_element_type=F32)
    placed_hi, placed_lo = split(placed)
    nothing = jnp.zeros((EDGE, depth), BF16)
    for pair in range(pairs):
        for piece, source in enumerate((placed_hi, placed_hi, placed_lo)):
            for h in range(PAIR):
                f = pair * PAIR + h
                at = (piece * PAIR + h) * EDGE
                for lanes in range(PAIR):
                    what = source[:, f * depth : (f + 1) * depth] if lanes == h else nothing
                    filt[pair, at : at + EDGE, lanes * depth : (lanes + 1) * depth] = what

    copy_coef.wait()
    swapped[...] = swap_in_blocks(coef[...].reshape(slots * EDGE, CUBE).astype(F32)).astype(BF16)

    span = PAIR * EDGE

    def synthesize(pair, carry):
        part = swapped[pl.ds(pl.multiple_of(pair * span, span), span), :]
        part = jnp.concatenate([part, part, part], axis=0)
        inner = dot_nt(kron_hi[...], part) + dot_nt(kron_lo[...], part)
        high = inner.astype(BF16).astype(F32)
        where = iota(inner.shape, 1)
        packed = jnp.where((where >= span) & (where < 2 * span), inner - high, high).astype(BF16)
        values = dot(packed, filt[pair])
        for h in range(PAIR):
            f = pair * PAIR + h
            value = values[:, h * depth : (h + 1) * depth]
            psi[f] = value
            weight = jnp.where(f < live_ref[0], occ_ref[f], 0.0)
            square = value * value * weight
            for a in range(EDGE):
                padded[f, pl.ds(stride * (a + 1) + rows_y, EDGE), :] = square[a * EDGE : (a + 1) * EDGE, :]
        return carry

    lax.fori_loop(0, pairs, synthesize, 0)

    def sum_plane(x):
        total = jnp.zeros((wide_y, depth), F32)
        for f in range(slots):
            corner_x, corner_y = corner(f)
            start = jnp.clip(x - corner_x + 1, 0, EDGE + 1) * stride + rows_y - corner_y
            total = total + padded[f, pl.ds(start, wide_y), :]
        partial[x] = total

    def sum_planes(first, count):
        def body(step, carry):
            sum_plane(first + step)
            return carry

        lax.fori_loop(0, count, body, 0)

    groups = REACH // GROUP
    all_groups = rows_x // GROUP

    def send(src, dst, sends, recvs, index, device):
        return pltpu.make_async_remote_copy(
            src_ref=src, dst_ref=dst, send_sem=sends.at[index], recv_sem=recvs.at[index],
            device_id=device, device_id_type=MESH,
        )

    first = {}
    for g in range(all_groups):
        here = pl.ds(g * GROUP, GROUP)
        if g < groups:
            there = pl.ds(rows_x + g * GROUP, GROUP)
            sum_planes(rows_x + g * GROUP, GROUP)
        sum_planes(g * GROUP, GROUP)
        if g == 0:
            pl.semaphore_wait(barrier, 6)
        copies = [send(partial.at[here, pl.ds(rows_y, EDGE)], from_y.at[here], send1, recv1, 3 * g, (gx, next_y))]
        if g < groups:
            copies.append(send(
                partial.at[there, pl.ds(rows_y, EDGE)], from_c.at[here], send1, recv1, 3 * g + 1, (next_x, next_y)))
            copies.append(send(
                partial.at[there, pl.ds(0, rows_y)], from_x.at[here], send1, recv1, 3 * g + 2, (next_x, yz)))
        for copy in copies:
            copy.start()
        first[g] = copies

    copy_core.wait()
    copy_vext.wait()

    second = {}
    out_copies = []
    for g in range(all_groups):
        here = pl.ds(g * GROUP, GROUP)
        for copy in first[g]:
            copy.wait_recv()
        density = core[here] + partial[here, pl.ds(0, rows_y), :]
        if g < groups:
            density = density + from_x[here]
            edge = density[:, :EDGE] + (from_y[here] + from_c[here])
        else:
            edge = density[:, :EDGE] + from_y[here]
        density = jnp.concatenate([edge, density[:, EDGE:]], axis=1)
        ext[here, pl.ds(0, rows_y), :] = vext[here] + XC_COEF * jnp.exp2(jnp.log2(density) * (1.0 / 3.0))
        copies = [send(ext.at[here, pl.ds(0, EDGE)], ext.at[here, pl.ds(rows_y, EDGE)], send2, recv2, 3 * g, (gx, last_y))]
        if g < groups:
            there = pl.ds(rows_x + g * GROUP, GROUP)
            copies.append(send(
                ext.at[here, pl.ds(0, EDGE)], ext.at[there, pl.ds(rows_y, EDGE)], send2, recv2, 3 * g + 1,
                (last_x, last_y)))
            copies.append(send(
                ext.at[here, pl.ds(0, rows_y)], ext.at[there, pl.ds(0, rows_y)], send2, recv2, 3 * g + 2, (last_x, yz)))
        for copy in copies:
            copy.start()
        second[g] = copies
        out = pltpu.make_async_copy(ext.at[here, pl.ds(0, rows_y)], pot_hbm.at[here], out_sems.at[g])
        out.start()
        out_copies.append(out)

    for g in range(all_groups):
        for copy in second[g]:
            copy.wait_recv()

    def analyze(pair, carry):
        parts = []
        for h in range(PAIR):
            f = pair * PAIR + h
            x, y = corner(f)
            box = ext[pl.ds(x, EDGE), pl.ds(y, EDGE), :].reshape(CUBE, depth)
            parts.append(box * psi[f])
        high, low = split(jnp.concatenate(parts, axis=1))
        left = filt[pair]
        both = dot_nt(left[span:], high)
        inner = both[:span] + both[span:] + dot_nt(left[:span], low)
        back[pl.ds(pl.multiple_of(pair * span, span), span), :] = inner
        return carry

    lax.fori_loop(0, pairs, analyze, 0)
    high, low = split(back[...])
    result = dot(high, kron_hi[...]) + (dot(high, kron_lo[...]) + dot(low, kron_hi[...]))
    result = swap_in_blocks(result)
    used = iota(result.shape, 0) < live_ref[0] * EDGE
    result = jnp.where(used, result, 0.0)
    hpsi_ref[...] = result.astype(BF16).reshape(slots, EDGE, CUBE)

    for g in range(all_groups):
        for copy in first[g] + second[g]:
            copy.wait_send()
        out_copies[g].wait()


def shards(n_gx, n_yz, coeffs, occupation, box_offset, live_count, synthesis, v_ext, core_density):
    slots = coeffs.shape[0]
    rows_x, rows_y, depth = v_ext.shape
    wide_x, wide_y = rows_x + EDGE, rows_y + EDGE
    exchanges = 3 * (rows_x // GROUP)
    smem = pl.BlockSpec(memory_space=pltpu.SMEM)
    vmem = pl.BlockSpec(memory_space=pltpu.VMEM)
    anywhere = pl.BlockSpec(memory_space=pl.ANY)
    return pl.pallas_call(
        functools.partial(kernel, (slots, rows_x, rows_y, depth, n_gx, n_yz)),
        out_shape=(
            jax.ShapeDtypeStruct(coeffs.shape, BF16),
            jax.ShapeDtypeStruct(v_ext.shape, F32),
        ),
        in_specs=[smem, smem, smem, vmem, anywhere, anywhere, anywhere],
        out_specs=(vmem, anywhere),
        scratch_shapes=[
            pltpu.VMEM(coeffs.shape, BF16),
            pltpu.VMEM(v_ext.shape, F32),
            pltpu.VMEM(v_ext.shape, F32),
            pltpu.VMEM((slots * EDGE, CUBE), BF16),
            pltpu.VMEM((CUBE, CUBE), BF16),
            pltpu.VMEM((CUBE, CUBE), BF16),
            pltpu.VMEM((slots // PAIR, 3 * PAIR * EDGE, PAIR * depth), BF16),
            pltpu.VMEM((slots, CUBE, depth), F32),
            pltpu.VMEM((slots, wide_y * (EDGE + 2) + rows_y, depth), F32),
            pltpu.VMEM((wide_x, wide_y, depth), F32),
            pltpu.VMEM((REACH, rows_y, depth), F32),
            pltpu.VMEM((rows_x, EDGE, depth), F32),
            pltpu.VMEM((REACH, EDGE, depth), F32),
            pltpu.VMEM((wide_x, wide_y, depth), F32),
            pltpu.VMEM((slots * EDGE, CUBE), F32),
            pltpu.SemaphoreType.DMA((3,)),
            pltpu.SemaphoreType.DMA((rows_x // GROUP,)),
            pltpu.SemaphoreType.DMA((exchanges,)),
            pltpu.SemaphoreType.DMA((exchanges,)),
            pltpu.SemaphoreType.DMA((exchanges,)),
            pltpu.SemaphoreType.DMA((exchanges,)),
        ],
        compiler_params=pltpu.CompilerParams(
            collective_id=0, has_side_effects=True, vmem_limit_bytes=40 * 1024 * 1024
        ),
    )(occupation, box_offset, live_count, synthesis, coeffs, v_ext, core_density)


def solution(mesh):
    placed = (
        P(("gx", "yz"), None, None),
        P(("gx", "yz")),
        P(("gx", "yz"), None),
        P(("gx", "yz")),
        P(),
        P("gx", "yz", None),
        P("gx", "yz", None),
    )
    return jax.shard_map(
        functools.partial(shards, mesh.shape["gx"], mesh.shape["yz"]),
        mesh=mesh,
        in_specs=placed,
        out_specs=(P(("gx", "yz"), None, None), P("gx", "yz", None)),
        check_vma=False,
    )
```

```python
import functools

import jax
import jax.numpy as jnp
from jax import lax
from jax.experimental import pallas as pl
from jax.experimental.pallas import tpu as pltpu
from jax.sharding import PartitionSpec as P

XC_COEF = -0.9847450218426964
EDGE = 16
CUBE = EDGE * EDGE
REACH = EDGE - 1
PAIR = 4
GROUP = 5
F32 = jnp.float32
BF16 = jnp.bfloat16
HIGHEST = lax.Precision.HIGHEST
MESH = pl.DeviceIdType.MESH


def iota(shape, dim):
    return lax.broadcasted_iota(jnp.int32, shape, dim)


def split(value):
    high = value.astype(BF16)
    low = (value - high.astype(F32)).astype(BF16)
    return high, low


def dot(left, right):
    return lax.dot_general(left, right, (((1,), (0,)), ((), ())), preferred_element_type=F32)


def dot_nt(left, right):
    return lax.dot_general(left, right, (((1,), (1,)), ((), ())), preferred_element_type=F32)


def swap_in_blocks(value):
    halves = []
    for half in range(CUBE // 128):
        part = value[:, half * 128 : (half + 1) * 128].reshape(CUBE // 8, 8, 128)
        row, col = iota(part.shape, 1), iota(part.shape, 2)
        for step in (1, 2, 4):
            up = pltpu.roll(pltpu.roll(part, 8 - step, 1), step, 2)
            down = pltpu.roll(pltpu.roll(part, step, 1), 128 - step, 2)
            moved = jnp.where((row & step) != 0, down, up)
            part = jnp.where(((row ^ col) & step) == 0, part, moved)
        part = part.reshape(EDGE, 2, 8, 128)
        first, second = part[:, 0], part[:, 1]
        far = (iota(first.shape, 2) & 8) != 0
        new_first = jnp.where(far, pltpu.roll(second, 8, 2), first)
        new_second = jnp.where(far, second, pltpu.roll(first, 120, 2))
        halves.append(jnp.stack([new_first, new_second], axis=1).reshape(CUBE, 128))
    return jnp.concatenate(halves, axis=1)


def kernel(
    sizes,
    occ_hbm, off_hbm, live, syn_hbm, coef_hbm, vext_hbm, core_hbm,
    hpsi_ref, ext,
    occ, off, off_rows, syn_ref, coef, vext, core, start_rows, starts,
    swapped, kron_hi, kron_lo, filt, psi, padded, partial, from_x, from_y, back,
    in_sems, table_sem, send_sems, recv_sems,
):
    slots, rows_x, rows_y, depth, n_gx, n_yz = sizes
    gx, yz = lax.axis_index("gx"), lax.axis_index("yz")
    wide_y = rows_y + EDGE
    stride = wide_y
    pairs = slots // PAIR

    inputs = (
        (coef_hbm, coef), (off_hbm, off), (off_hbm, off_rows), (syn_hbm, syn_ref), (occ_hbm, occ),
        (core_hbm, core), (vext_hbm, vext),
    )
    loads = [pltpu.make_async_copy(src, dst, in_sems.at[n]) for n, (src, dst) in enumerate(inputs)]
    for load in loads:
        load.start()
    load_coef, load_off, load_off_rows, load_syn, load_occ, load_core, load_vext = loads

    after_x, before_x = gx < n_gx - 1, gx > 0
    after_y, before_y = yz < n_yz - 1, yz > 0
    next_x, next_y, last_x, last_y = (gx + 1, yz), (gx, yz + 1), (gx - 1, yz), (gx, yz - 1)
    barrier = pltpu.get_barrier_semaphore()
    neighbours = 0
    for there, device in ((after_x, next_x), (after_y, next_y), (before_x, last_x), (before_y, last_y)):
        @pl.when(there)
        def _(device=device):
            pl.semaphore_signal(barrier, inc=1, device_id=device, device_id_type=MESH)

        neighbours = neighbours + there.astype(jnp.int32)

    @pl.when(jnp.logical_not(before_x))
    def _():
        from_x[...] = jnp.zeros_like(from_x)

    @pl.when(jnp.logical_not(before_y))
    def _():
        from_y[...] = jnp.zeros_like(from_y)

    def clear(slot, carry):
        for plane in range(EDGE + 3):
            padded[slot, pl.ds(stride * plane, rows_y), :] = jnp.zeros((rows_y, depth), F32)
        for plane in (0, EDGE + 1):
            padded[slot, pl.ds(stride * plane + rows_y, EDGE), :] = jnp.zeros((EDGE, depth), F32)
        return carry

    lax.fori_loop(0, slots, clear, 0)

    load_off_rows.wait()
    begin_x = jnp.clip(off_rows[0:1, :] - gx * rows_x, 0, rows_x - 1)
    begin_y = jnp.clip(off_rows[1:2, :] - yz * rows_y, 0, rows_y - 1)
    plane = jnp.clip(iota((rows_x + EDGE, slots), 0) - begin_x + 1, 0, EDGE + 1)
    start_rows[:, :slots] = plane * stride + rows_y - begin_y
    table = pltpu.make_async_copy(start_rows, starts, table_sem)
    table.start()

    load_syn.wait()
    syn = syn_ref[...]
    lane = iota((EDGE, CUBE), 1)
    row = iota((EDGE, CUBE), 0)
    by_i = lax.dot(syn, (lane % EDGE == row).astype(F32), precision=HIGHEST, preferred_element_type=F32)
    by_j = lax.dot(syn, (lane // EDGE == row).astype(F32), precision=HIGHEST, preferred_element_type=F32)
    for a in range(EDGE):
        high, low = split(by_i[a : a + 1, :] * by_j)
        kron_hi[a * EDGE : (a + 1) * EDGE, :] = high
        kron_lo[a * EDGE : (a + 1) * EDGE, :] = low

    load_off.wait()
    load_occ.wait()
    shift = iota((EDGE, depth), 1) - iota((EDGE, depth), 0)
    places = jnp.concatenate([(shift == off[2, f]).astype(F32) for f in range(slots)], axis=1)
    placed = lax.dot_general(syn, places, (((0,), (0,)), ((), ())), precision=HIGHEST, preferred_element_type=F32)
    placed_hi, placed_lo = split(placed)
    nothing = jnp.zeros((EDGE, depth), BF16)
    for pair in range(pairs):
        for piece, source in enumerate((placed_hi, placed_hi, placed_lo)):
            for h in range(PAIR):
                f = pair * PAIR + h
                at = (piece * PAIR + h) * EDGE
                for lanes in range(PAIR):
                    what = source[:, f * depth : (f + 1) * depth] if lanes == h else nothing
                    filt[pair, at : at + EDGE, lanes * depth : (lanes + 1) * depth] = what

    def corner(f):
        x = jnp.clip(off[0, f] - gx * rows_x, 0, rows_x - 1)
        y = jnp.clip(off[1, f] - yz * rows_y, 0, rows_y - 1)
        return x, y

    load_coef.wait()
    swapped[...] = swap_in_blocks(coef[...].reshape(slots * EDGE, CUBE).astype(F32)).astype(BF16)

    span = PAIR * EDGE

    def synthesize(pair, carry):
        part = swapped[pl.ds(pl.multiple_of(pair * span, span), span), :]
        part = jnp.concatenate([part, part, part], axis=0)
        inner = dot_nt(kron_hi[...], part) + dot_nt(kron_lo[...], part)
        high = inner.astype(BF16).astype(F32)
        where = iota(inner.shape, 1)
        packed = jnp.where((where >= span) & (where < 2 * span), inner - high, high).astype(BF16)
        values = dot(packed, filt[pair])
        for h in range(PAIR):
            f = pair * PAIR + h
            value = values[:, h * depth : (h + 1) * depth]
            psi[f] = value
            weight = jnp.where(f < live[0], occ[f], 0.0)
            square = value * value * weight
            for a in range(EDGE):
                padded[f, pl.ds(stride * (a + 1) + rows_y, EDGE), :] = square[a * EDGE : (a + 1) * EDGE, :]
        return carry

    lax.fori_loop(0, pairs, synthesize, 0)

    def sum_planes(first, count, unit):
        def body(step, carry):
            x = first + step * unit
            totals = [None] * unit
            for f in range(slots):
                for n in range(unit):
                    rows = padded[f, pl.ds(starts[x + n, f], wide_y), :]
                    totals[n] = rows if f == 0 else totals[n] + rows
            for n in range(unit):
                partial[x + n] = totals[n]
            return carry

        lax.fori_loop(0, count // unit, body, 0)

    table.wait()
    issued = []

    def copy(there, src, dst, device, arrives):
        index = len(issued)
        descriptor = pltpu.make_async_remote_copy(
            src_ref=src, dst_ref=dst, send_sem=send_sems.at[index], recv_sem=recv_sems.at[index],
            device_id=device, device_id_type=MESH,
        )

        @pl.when(there)
        def _():
            descriptor.start()

        issued.append((there, descriptor))

        def landed():
            @pl.when(arrives)
            def _():
                descriptor.wait_recv()

        return landed

    groups = REACH // GROUP
    rest = rows_x - REACH
    near, far = pl.ds(0, rows_y), pl.ds(rows_y, EDGE)
    edge, inner = pl.ds(0, EDGE), pl.ds(EDGE, rows_y - EDGE)
    spans = [pl.ds(g * GROUP, GROUP) for g in range(groups)]
    beyond = [pl.ds(rows_x + g * GROUP, GROUP) for g in range(groups)]
    others = pl.ds(REACH, rest)

    corner_in, main_in, side_in = [], [], []
    for g in range(groups):
        sum_planes(rows_x + g * GROUP, GROUP, GROUP)
        if g == 0:
            pl.semaphore_wait(barrier, neighbours)
        corner_in.append(copy(after_x, partial.at[beyond[g], far], from_x.at[spans[g], far], next_x, before_x))
    sum_planes(REACH, rest, 3)
    rest_in = copy(after_y, partial.at[others, far], from_y.at[others], next_y, before_y)
    for g in range(groups):
        main_in.append(copy(after_x, partial.at[beyond[g], near], from_x.at[spans[g], near], next_x, before_x))
    sum_planes(0, REACH, GROUP)
    for g in range(groups):
        corner_in[g]()
        partial[spans[g], far, :] += from_x[spans[g], far, :]
        side_in.append(copy(after_y, partial.at[spans[g], far], from_y.at[spans[g]], next_y, before_y))

    def apply(planes, along_x, along_y):
        rows = edge if along_y else inner
        density = core[planes, rows, :] + partial[planes, rows, :]
        if along_x:
            density = density + from_x[planes, rows, :]
        if along_y:
            density = density + from_y[planes]
        ext[planes, rows, :] = vext[planes, rows, :] + XC_COEF * jnp.exp2(jnp.log2(density) * (1.0 / 3.0))

    load_core.wait()
    load_vext.wait()
    rest_in()
    apply(others, False, True)
    apply(others, False, False)
    waits = [copy(before_y, ext.at[others, edge], ext.at[others, far], last_y, after_y)]
    back_in = []
    for g in range(groups):
        main_in[g]()
        apply(spans[g], True, False)
        waits.append(copy(before_x, ext.at[spans[g], inner], ext.at[beyond[g], inner], last_x, after_x))
    for g in range(groups):
        side_in[g]()
        apply(spans[g], True, True)
        back_in.append(copy(before_y, ext.at[spans[g], edge], ext.at[spans[g], far], last_y, after_y))
        waits.append(copy(before_x, ext.at[spans[g], edge], ext.at[beyond[g], edge], last_x, after_x))
    for g in range(groups):
        back_in[g]()
        waits.append(copy(
            before_x & after_y, ext.at[spans[g], far], ext.at[beyond[g], far], last_x, after_x & after_y))
    for landed in waits:
        landed()

    def analyze(pair, carry):
        parts = []
        for h in range(PAIR):
            f = pair * PAIR + h
            x, y = corner(f)
            box = ext[pl.ds(x, EDGE), pl.ds(y, EDGE), :].reshape(CUBE, depth)
            parts.append(box * psi[f])
        high, low = split(jnp.concatenate(parts, axis=1))
        left = filt[pair]
        both = dot_nt(left[span:], high)
        inner = both[:span] + both[span:] + dot_nt(left[:span], low)
        back[pl.ds(pl.multiple_of(pair * span, span), span), :] = inner
        return carry

    lax.fori_loop(0, pairs, analyze, 0)
    high, low = split(back[...])
    result = dot(high, kron_hi[...]) + (dot(high, kron_lo[...]) + dot(low, kron_hi[...]))
    result = swap_in_blocks(result)
    used = iota(result.shape, 0) < live[0] * EDGE
    result = jnp.where(used, result, 0.0)
    hpsi_ref[...] = result.astype(BF16).reshape(slots, EDGE, CUBE)

    for there, descriptor in issued:
        @pl.when(there)
        def _(descriptor=descriptor):
            descriptor.wait_send()


def deliver(hpsi_ref, ext, hpsi_hbm, pot_hbm, sems):
    rows_x, rows_y, _ = pot_hbm.shape
    copies = (
        pltpu.make_async_copy(hpsi_ref, hpsi_hbm, sems.at[0]),
        pltpu.make_async_copy(ext.at[pl.ds(0, rows_x), pl.ds(0, rows_y)], pot_hbm, sems.at[1]),
    )
    for copy in copies:
        copy.start()
    for copy in copies:
        copy.wait()


def shards(n_gx, n_yz, coeffs, occupation, box_offset, live_count, synthesis, v_ext, core_density):
    slots = coeffs.shape[0]
    rows_x, rows_y, depth = v_ext.shape
    wide_x, wide_y = rows_x + EDGE, rows_y + EDGE
    exchanges = 2 + 7 * (REACH // GROUP)
    vmem = pl.BlockSpec(memory_space=pltpu.VMEM)
    hbm = pl.BlockSpec(memory_space=pltpu.HBM)
    inputs = (occupation, box_offset.T, live_count, synthesis, coeffs, v_ext, core_density)
    hpsi, ext = pl.pallas_call(
        functools.partial(kernel, (slots, rows_x, rows_y, depth, n_gx, n_yz)),
        out_shape=(pltpu.VMEM(coeffs.shape, BF16), pltpu.VMEM((wide_x, wide_y, depth), F32)),
        in_specs=[hbm, hbm, pl.BlockSpec(memory_space=pltpu.SMEM), hbm, hbm, hbm, hbm],
        out_specs=(vmem, vmem),
        scratch_shapes=[
            pltpu.SMEM(occupation.shape, F32),
            pltpu.SMEM((3, slots), jnp.int32),
            pltpu.VMEM((3, slots), jnp.int32),
            pltpu.VMEM(synthesis.shape, F32),
            pltpu.VMEM(coeffs.shape, BF16),
            pltpu.VMEM(v_ext.shape, F32),
            pltpu.VMEM(v_ext.shape, F32),
            pltpu.VMEM((wide_x, 128), jnp.int32),
            pltpu.SMEM((wide_x, 128), jnp.int32),
            pltpu.VMEM((slots * EDGE, CUBE), BF16),
            pltpu.VMEM((CUBE, CUBE), BF16),
            pltpu.VMEM((CUBE, CUBE), BF16),
            pltpu.VMEM((slots // PAIR, 3 * PAIR * EDGE, PAIR * depth), BF16),
            pltpu.VMEM((slots, CUBE, depth), F32),
            pltpu.VMEM((slots, wide_y * (EDGE + 2) + rows_y, depth), F32),
            pltpu.VMEM((wide_x, wide_y, depth), F32),
            pltpu.VMEM((REACH, wide_y, depth), F32),
            pltpu.VMEM((rows_x, EDGE, depth), F32),
            pltpu.VMEM((slots * EDGE, CUBE), F32),
            pltpu.SemaphoreType.DMA((len(inputs),)),
            pltpu.SemaphoreType.DMA,
            pltpu.SemaphoreType.DMA((exchanges,)),
            pltpu.SemaphoreType.DMA((exchanges,)),
        ],
        compiler_params=pltpu.CompilerParams(
            collective_id=0, has_side_effects=True, vmem_limit_bytes=40 * 1024 * 1024
        ),
    )(*(v if v is live_count else pltpu.with_memory_space_constraint(v, pltpu.HBM) for v in inputs))
    return pl.pallas_call(
        deliver,
        out_shape=(jax.ShapeDtypeStruct(coeffs.shape, BF16), jax.ShapeDtypeStruct(v_ext.shape, F32)),
        in_specs=[vmem, vmem],
        out_specs=(hbm, hbm),
        scratch_shapes=[pltpu.SemaphoreType.DMA((2,))],
        compiler_params=pltpu.CompilerParams(vmem_limit_bytes=16 * 1024 * 1024),
    )(hpsi, ext)


def solution(mesh):
    placed = (
        P(("gx", "yz"), None, None),
        P(("gx", "yz")),
        P(("gx", "yz"), None),
        P(("gx", "yz")),
        P(),
        P("gx", "yz", None),
        P("gx", "yz", None),
    )
    return jax.shard_map(
        functools.partial(shards, mesh.shape["gx"], mesh.shape["yz"]),
        mesh=mesh,
        in_specs=placed,
        out_specs=(P(("gx", "yz"), None, None), P("gx", "yz", None)),
        check_vma=False,
    )
```

```python
import functools

import jax
import jax.numpy as jnp
from jax import lax
from jax.experimental import pallas as pl
from jax.experimental.pallas import tpu as pltpu
from jax.sharding import PartitionSpec as P

XC_COEF = -0.9847450218426964
EDGE = 16
CUBE = EDGE * EDGE
REACH = EDGE - 1
PAIR = 4
GROUP = 5
F32 = jnp.float32
BF16 = jnp.bfloat16
HIGHEST = lax.Precision.HIGHEST
MESH = pl.DeviceIdType.MESH


def iota(shape, dim):
    return lax.broadcasted_iota(jnp.int32, shape, dim)


def split(value):
    high = value.astype(BF16)
    low = (value - high.astype(F32)).astype(BF16)
    return high, low


def dot(left, right):
    return lax.dot_general(left, right, (((1,), (0,)), ((), ())), preferred_element_type=F32)


def dot_nt(left, right):
    return lax.dot_general(left, right, (((1,), (1,)), ((), ())), preferred_element_type=F32)


def swap_in_blocks(value):
    halves = []
    for half in range(CUBE // 128):
        part = value[:, half * 128 : (half + 1) * 128].reshape(CUBE // 8, 8, 128)
        row, col = iota(part.shape, 1), iota(part.shape, 2)
        for step in (1, 2, 4):
            up = pltpu.roll(pltpu.roll(part, 8 - step, 1), step, 2)
            down = pltpu.roll(pltpu.roll(part, step, 1), 128 - step, 2)
            moved = jnp.where((row & step) != 0, down, up)
            part = jnp.where(((row ^ col) & step) == 0, part, moved)
        part = part.reshape(EDGE, 2, 8, 128)
        first, second = part[:, 0], part[:, 1]
        far = (iota(first.shape, 2) & 8) != 0
        new_first = jnp.where(far, pltpu.roll(second, 8, 2), first)
        new_second = jnp.where(far, second, pltpu.roll(first, 120, 2))
        halves.append(jnp.stack([new_first, new_second], axis=1).reshape(CUBE, 128))
    return jnp.concatenate(halves, axis=1)


def kernel(
    sizes,
    occ_hbm, off_hbm, live, syn_hbm, coef_hbm, vext_hbm, core_hbm,
    hpsi_ref, ext,
    occ, off, off_rows, syn_ref, coef, vext, core, start_rows, starts,
    swapped, kron_hi, kron_lo, filt, psi, padded, partial, from_x, from_y, from_after, vext_far, back,
    in_sems, table_sem, send_sems, recv_sems,
):
    slots, rows_x, rows_y, depth, n_gx, n_yz = sizes
    gx, yz = lax.axis_index("gx"), lax.axis_index("yz")
    wide_y = rows_y + EDGE
    stride = wide_y
    pairs = slots // PAIR

    inputs = (
        (coef_hbm, coef), (off_hbm, off), (off_hbm, off_rows), (syn_hbm, syn_ref), (occ_hbm, occ),
        (core_hbm, core), (vext_hbm, vext),
    )
    loads = [pltpu.make_async_copy(src, dst, in_sems.at[n]) for n, (src, dst) in enumerate(inputs)]
    for load in loads:
        load.start()
    load_coef, load_off, load_off_rows, load_syn, load_occ, load_core, load_vext = loads

    after_x, before_x = gx < n_gx - 1, gx > 0
    after_y, before_y = yz < n_yz - 1, yz > 0
    next_x, next_y, last_x, last_y = (gx + 1, yz), (gx, yz + 1), (gx - 1, yz), (gx, yz - 1)
    barrier = pltpu.get_barrier_semaphore()
    neighbours = 0
    for there, device in ((after_x, next_x), (after_y, next_y), (before_x, last_x), (before_y, last_y)):
        @pl.when(there)
        def _(device=device):
            pl.semaphore_signal(barrier, inc=1, device_id=device, device_id_type=MESH)

        neighbours = neighbours + there.astype(jnp.int32)

    @pl.when(jnp.logical_not(before_x))
    def _():
        from_x[...] = jnp.zeros_like(from_x)

    @pl.when(jnp.logical_not(before_y))
    def _():
        from_y[...] = jnp.zeros_like(from_y)

    @pl.when(jnp.logical_not(after_y))
    def _():
        from_after[...] = jnp.zeros_like(from_after)
        vext_far[...] = jnp.zeros_like(vext_far)

    def clear(slot, carry):
        for plane in range(EDGE + 3):
            padded[slot, pl.ds(stride * plane, rows_y), :] = jnp.zeros((rows_y, depth), F32)
        for plane in (0, EDGE + 1):
            padded[slot, pl.ds(stride * plane + rows_y, EDGE), :] = jnp.zeros((EDGE, depth), F32)
        return carry

    lax.fori_loop(0, slots, clear, 0)

    load_off_rows.wait()
    begin_x = jnp.clip(off_rows[0:1, :] - gx * rows_x, 0, rows_x - 1)
    begin_y = jnp.clip(off_rows[1:2, :] - yz * rows_y, 0, rows_y - 1)
    plane = jnp.clip(iota((rows_x + EDGE, slots), 0) - begin_x + 1, 0, EDGE + 1)
    start_rows[:, :slots] = plane * stride + rows_y - begin_y
    table = pltpu.make_async_copy(start_rows, starts, table_sem)
    table.start()

    load_syn.wait()
    syn = syn_ref[...]
    lane = iota((EDGE, CUBE), 1)
    row = iota((EDGE, CUBE), 0)
    by_i = lax.dot(syn, (lane % EDGE == row).astype(F32), precision=HIGHEST, preferred_element_type=F32)
    by_j = lax.dot(syn, (lane // EDGE == row).astype(F32), precision=HIGHEST, preferred_element_type=F32)
    for a in range(EDGE):
        high, low = split(by_i[a : a + 1, :] * by_j)
        kron_hi[a * EDGE : (a + 1) * EDGE, :] = high
        kron_lo[a * EDGE : (a + 1) * EDGE, :] = low

    load_off.wait()
    load_occ.wait()
    shift = iota((EDGE, depth), 1) - iota((EDGE, depth), 0)
    places = jnp.concatenate([(shift == off[2, f]).astype(F32) for f in range(slots)], axis=1)
    placed = lax.dot_general(syn, places, (((0,), (0,)), ((), ())), precision=HIGHEST, preferred_element_type=F32)
    placed_hi, placed_lo = split(placed)
    nothing = jnp.zeros((EDGE, depth), BF16)
    for pair in range(pairs):
        for piece, source in enumerate((placed_hi, placed_hi, placed_lo)):
            for h in range(PAIR):
                f = pair * PAIR + h
                at = (piece * PAIR + h) * EDGE
                for lanes in range(PAIR):
                    what = source[:, f * depth : (f + 1) * depth] if lanes == h else nothing
                    filt[pair, at : at + EDGE, lanes * depth : (lanes + 1) * depth] = what

    def corner(f):
        x = jnp.clip(off[0, f] - gx * rows_x, 0, rows_x - 1)
        y = jnp.clip(off[1, f] - yz * rows_y, 0, rows_y - 1)
        return x, y

    load_coef.wait()
    swapped[...] = swap_in_blocks(coef[...].reshape(slots * EDGE, CUBE).astype(F32)).astype(BF16)

    span = PAIR * EDGE

    def synthesize(pair, carry):
        part = swapped[pl.ds(pl.multiple_of(pair * span, span), span), :]
        part = jnp.concatenate([part, part, part], axis=0)
        inner = dot_nt(kron_hi[...], part) + dot_nt(kron_lo[...], part)
        high = inner.astype(BF16).astype(F32)
        where = iota(inner.shape, 1)
        packed = jnp.where((where >= span) & (where < 2 * span), inner - high, high).astype(BF16)
        values = dot(packed, filt[pair])
        for h in range(PAIR):
            f = pair * PAIR + h
            value = values[:, h * depth : (h + 1) * depth]
            psi[f] = value
            weight = jnp.where(f < live[0], occ[f], 0.0)
            square = value * value * weight
            for a in range(EDGE):
                padded[f, pl.ds(stride * (a + 1) + rows_y, EDGE), :] = square[a * EDGE : (a + 1) * EDGE, :]
        return carry

    issued = []

    def copy(there, src, dst, device, arrives):
        index = len(issued)
        descriptor = pltpu.make_async_remote_copy(
            src_ref=src, dst_ref=dst, send_sem=send_sems.at[index], recv_sem=recv_sems.at[index],
            device_id=device, device_id_type=MESH,
        )

        @pl.when(there)
        def _():
            descriptor.start()

        issued.append((there, descriptor))

        def landed():
            @pl.when(arrives)
            def _():
                descriptor.wait_recv()

        return landed

    groups = REACH // GROUP
    rest = rows_x - REACH
    edge, inner, far = pl.ds(0, EDGE), pl.ds(EDGE, rows_y - EDGE), pl.ds(rows_y, EDGE)
    spans = [pl.ds(g * GROUP, GROUP) for g in range(groups)]
    beyond = [pl.ds(rows_x + g * GROUP, GROUP) for g in range(groups)]
    others = pl.ds(REACH, rest)

    pl.semaphore_wait(barrier, neighbours)
    vext_in = copy(before_y, vext_hbm.at[pl.ds(0, REACH), edge], vext_far, last_y, after_y)

    lax.fori_loop(0, pairs, synthesize, 0)

    def sum_planes(first, count, unit, own):
        def body(step, carry):
            x = first + step * unit
            totals = [None] * unit
            for f in range(slots):
                for n in range(unit):
                    rows = padded[f, pl.ds(starts[x + n, f], wide_y), :]
                    totals[n] = rows if f == 0 else totals[n] + rows
            for n in range(unit):
                if own:
                    partial[x + n, :rows_y, :] = totals[n][:rows_y] + core[x + n]
                    partial[x + n, rows_y:, :] = totals[n][rows_y:]
                else:
                    partial[x + n] = totals[n]
            return carry

        lax.fori_loop(0, count // unit, body, 0)

    table.wait()

    far_in, edge_in, inner_in = [], [], []
    for g in range(groups):
        sum_planes(rows_x + g * GROUP, GROUP, GROUP, False)
        far_in.append(copy(after_x, partial.at[beyond[g], far], from_x.at[spans[g], far], next_x, before_x))
        edge_in.append(copy(after_x, partial.at[beyond[g], edge], from_x.at[spans[g], edge], next_x, before_x))
    load_core.wait()
    sum_planes(REACH, rest, 3, True)
    rest_in = copy(after_y, partial.at[others, far], from_y.at[others], next_y, before_y)
    for g in range(groups):
        inner_in.append(copy(after_x, partial.at[beyond[g], inner], from_x.at[spans[g], inner], next_x, before_x))
    sum_planes(0, REACH, GROUP, True)

    onward_in, back_in = [], []
    for g in range(groups):
        far_in[g]()
        partial[spans[g], far, :] += from_x[spans[g], far, :]
        onward_in.append(copy(after_y, partial.at[spans[g], far], from_y.at[spans[g]], next_y, before_y))
        edge_in[g]()
        partial[spans[g], edge, :] += from_x[spans[g], edge, :]
        back_in.append(copy(before_y, partial.at[spans[g], edge], from_after.at[spans[g]], last_y, after_y))

    def potential(planes, rows, external, *densities):
        density = functools.reduce(jnp.add, densities)
        ext[planes, rows, :] = external + XC_COEF * jnp.exp2(jnp.log2(density) * (1.0 / 3.0))

    load_vext.wait()
    waits = []
    for g in range(groups):
        inner_in[g]()
        potential(spans[g], inner, vext[spans[g], inner, :], partial[spans[g], inner, :], from_x[spans[g], inner, :])
        waits.append(copy(before_x, ext.at[spans[g], inner], ext.at[beyond[g], inner], last_x, after_x))
    rest_in()
    potential(others, edge, vext[others, edge, :], partial[others, edge, :], from_y[others])
    waits.append(copy(before_y, ext.at[others, edge], ext.at[others, far], last_y, after_y))
    potential(others, inner, vext[others, inner, :], partial[others, inner, :])
    vext_in()
    for g in range(groups):
        onward_in[g]()
        potential(spans[g], edge, vext[spans[g], edge, :], partial[spans[g], edge, :], from_y[spans[g]])
        waits.append(copy(before_x, ext.at[spans[g], edge], ext.at[beyond[g], edge], last_x, after_x))
        back_in[g]()
        potential(spans[g], far, vext_far[spans[g]], partial[spans[g], far, :], from_after[spans[g]])
        waits.append(copy(before_x, ext.at[spans[g], far], ext.at[beyond[g], far], last_x, after_x))
    for landed in waits:
        landed()

    def analyze(pair, carry):
        parts = []
        for h in range(PAIR):
            f = pair * PAIR + h
            x, y = corner(f)
            box = ext[pl.ds(x, EDGE), pl.ds(y, EDGE), :].reshape(CUBE, depth)
            parts.append(box * psi[f])
        high, low = split(jnp.concatenate(parts, axis=1))
        left = filt[pair]
        both = dot_nt(left[span:], high)
        inner = both[:span] + both[span:] + dot_nt(left[:span], low)
        back[pl.ds(pl.multiple_of(pair * span, span), span), :] = inner
        return carry

    lax.fori_loop(0, pairs, analyze, 0)
    high, low = split(back[...])
    result = dot(high, kron_hi[...]) + (dot(high, kron_lo[...]) + dot(low, kron_hi[...]))
    result = swap_in_blocks(result)
    used = iota(result.shape, 0) < live[0] * EDGE
    result = jnp.where(used, result, 0.0)
    hpsi_ref[...] = result.astype(BF16).reshape(slots, EDGE, CUBE)

    for there, descriptor in issued:
        @pl.when(there)
        def _(descriptor=descriptor):
            descriptor.wait_send()


def deliver(hpsi_ref, ext, hpsi_hbm, pot_hbm, sems):
    rows_x, rows_y, _ = pot_hbm.shape
    copies = (
        pltpu.make_async_copy(hpsi_ref, hpsi_hbm, sems.at[0]),
        pltpu.make_async_copy(ext.at[pl.ds(0, rows_x), pl.ds(0, rows_y)], pot_hbm, sems.at[1]),
    )
    for copy in copies:
        copy.start()
    for copy in copies:
        copy.wait()


def shards(n_gx, n_yz, coeffs, occupation, box_offset, live_count, synthesis, v_ext, core_density):
    slots = coeffs.shape[0]
    rows_x, rows_y, depth = v_ext.shape
    wide_x, wide_y = rows_x + EDGE, rows_y + EDGE
    exchanges = 3 + 8 * (REACH // GROUP)
    vmem = pl.BlockSpec(memory_space=pltpu.VMEM)
    hbm = pl.BlockSpec(memory_space=pltpu.HBM)
    inputs = (occupation, box_offset.T, live_count, synthesis, coeffs, v_ext, core_density)
    hpsi, ext = pl.pallas_call(
        functools.partial(kernel, (slots, rows_x, rows_y, depth, n_gx, n_yz)),
        out_shape=(pltpu.VMEM(coeffs.shape, BF16), pltpu.VMEM((wide_x, wide_y, depth), F32)),
        in_specs=[hbm, hbm, pl.BlockSpec(memory_space=pltpu.SMEM), hbm, hbm, hbm, hbm],
        out_specs=(vmem, vmem),
        scratch_shapes=[
            pltpu.SMEM(occupation.shape, F32),
            pltpu.SMEM((3, slots), jnp.int32),
            pltpu.VMEM((3, slots), jnp.int32),
            pltpu.VMEM(synthesis.shape, F32),
            pltpu.VMEM(coeffs.shape, BF16),
            pltpu.VMEM(v_ext.shape, F32),
            pltpu.VMEM(v_ext.shape, F32),
            pltpu.VMEM((wide_x, 128), jnp.int32),
            pltpu.SMEM((wide_x, 128), jnp.int32),
            pltpu.VMEM((slots * EDGE, CUBE), BF16),
            pltpu.VMEM((CUBE, CUBE), BF16),
            pltpu.VMEM((CUBE, CUBE), BF16),
            pltpu.VMEM((slots // PAIR, 3 * PAIR * EDGE, PAIR * depth), BF16),
            pltpu.VMEM((slots, CUBE, depth), F32),
            pltpu.VMEM((slots, wide_y * (EDGE + 2) + rows_y, depth), F32),
            pltpu.VMEM((wide_x, wide_y, depth), F32),
            pltpu.VMEM((REACH, wide_y, depth), F32),
            pltpu.VMEM((rows_x, EDGE, depth), F32),
            pltpu.VMEM((REACH, EDGE, depth), F32),
            pltpu.VMEM((REACH, EDGE, depth), F32),
            pltpu.VMEM((slots * EDGE, CUBE), F32),
            pltpu.SemaphoreType.DMA((len(inputs),)),
            pltpu.SemaphoreType.DMA,
            pltpu.SemaphoreType.DMA((exchanges,)),
            pltpu.SemaphoreType.DMA((exchanges,)),
        ],
        compiler_params=pltpu.CompilerParams(
            collective_id=0, has_side_effects=True, vmem_limit_bytes=40 * 1024 * 1024
        ),
    )(*(v if v is live_count else pltpu.with_memory_space_constraint(v, pltpu.HBM) for v in inputs))
    return pl.pallas_call(
        deliver,
        out_shape=(jax.ShapeDtypeStruct(coeffs.shape, BF16), jax.ShapeDtypeStruct(v_ext.shape, F32)),
        in_specs=[vmem, vmem],
        out_specs=(hbm, hbm),
        scratch_shapes=[pltpu.SemaphoreType.DMA((2,))],
        compiler_params=pltpu.CompilerParams(vmem_limit_bytes=16 * 1024 * 1024),
    )(hpsi, ext)


def solution(mesh):
    placed = (
        P(("gx", "yz"), None, None),
        P(("gx", "yz")),
        P(("gx", "yz"), None),
        P(("gx", "yz")),
        P(),
        P("gx", "yz", None),
        P("gx", "yz", None),
    )
    return jax.shard_map(
        functools.partial(shards, mesh.shape["gx"], mesh.shape["yz"]),
        mesh=mesh,
        in_specs=placed,
        out_specs=(P(("gx", "yz"), None, None), P("gx", "yz", None)),
        check_vma=False,
    )
```

```python
import functools

import jax
import jax.numpy as jnp
from jax import lax
from jax.experimental import pallas as pl
from jax.experimental.pallas import tpu as pltpu
from jax.sharding import PartitionSpec as P

XC_COEF = -0.9847450218426964
EDGE = 16
CUBE = EDGE * EDGE
REACH = EDGE - 1
PAIR = 4
GROUP = 5
F32 = jnp.float32
BF16 = jnp.bfloat16
HIGHEST = lax.Precision.HIGHEST
MESH = pl.DeviceIdType.MESH


def iota(shape, dim):
    return lax.broadcasted_iota(jnp.int32, shape, dim)


def split(value):
    high = value.astype(BF16)
    low = (value - high.astype(F32)).astype(BF16)
    return high, low


def dot(left, right):
    return lax.dot_general(left, right, (((1,), (0,)), ((), ())), preferred_element_type=F32)


def dot_nt(left, right):
    return lax.dot_general(left, right, (((1,), (1,)), ((), ())), preferred_element_type=F32)


def swap_in_blocks(value):
    halves = []
    for half in range(CUBE // 128):
        part = value[:, half * 128 : (half + 1) * 128].reshape(CUBE // 8, 8, 128)
        row, col = iota(part.shape, 1), iota(part.shape, 2)
        for step in (1, 2, 4):
            up = pltpu.roll(pltpu.roll(part, 8 - step, 1), step, 2)
            down = pltpu.roll(pltpu.roll(part, step, 1), 128 - step, 2)
            moved = jnp.where((row & step) != 0, down, up)
            part = jnp.where(((row ^ col) & step) == 0, part, moved)
        part = part.reshape(EDGE, 2, 8, 128)
        first, second = part[:, 0], part[:, 1]
        far = (iota(first.shape, 2) & 8) != 0
        new_first = jnp.where(far, pltpu.roll(second, 8, 2), first)
        new_second = jnp.where(far, second, pltpu.roll(first, 120, 2))
        halves.append(jnp.stack([new_first, new_second], axis=1).reshape(CUBE, 128))
    return jnp.concatenate(halves, axis=1)


def kernel(
    sizes,
    occ_hbm, off_hbm, live, syn_hbm, coef_hbm, vext_hbm, core_hbm,
    hpsi_ref, ext,
    occ, off, off_rows, syn_ref, coef, vext, core, start_rows, starts,
    swapped, kron_hi, kron_lo, filt, psi, padded, partial, from_x, from_y, from_after, vext_far,
    from_next, vext_next, vext_corner, side_far, side_edge, halo_far, halo_edge, halo_from_y, halo_from_after, back,
    in_sems, table_sem, send_sems, recv_sems,
):
    slots, rows_x, rows_y, depth, n_gx, n_yz = sizes
    gx, yz = lax.axis_index("gx"), lax.axis_index("yz")
    wide_y = rows_y + EDGE
    stride = wide_y
    pairs = slots // PAIR

    inputs = (
        (coef_hbm, coef), (off_hbm, off), (off_hbm, off_rows), (syn_hbm, syn_ref), (occ_hbm, occ),
        (core_hbm, core), (vext_hbm, vext),
    )
    loads = [pltpu.make_async_copy(src, dst, in_sems.at[n]) for n, (src, dst) in enumerate(inputs)]
    for load in loads:
        load.start()
    load_coef, load_off, load_off_rows, load_syn, load_occ, load_core, load_vext = loads

    after_x, before_x = gx < n_gx - 1, gx > 0
    after_y, before_y = yz < n_yz - 1, yz > 0
    next_x, next_y, last_x, last_y = (gx + 1, yz), (gx, yz + 1), (gx - 1, yz), (gx, yz - 1)
    odd = lax.rem(gx, 2) == 1
    even = jnp.logical_not(odd)
    alone, feeds, takes = odd & after_x, even & before_x, even & after_x
    barrier = pltpu.get_barrier_semaphore()
    neighbours = 0
    for there, device in ((after_x, next_x), (after_y, next_y), (before_x, last_x), (before_y, last_y)):
        @pl.when(there)
        def _(device=device):
            pl.semaphore_signal(barrier, inc=1, device_id=device, device_id_type=MESH)

        neighbours = neighbours + there.astype(jnp.int32)

    @pl.when(jnp.logical_not(before_x))
    def _():
        from_x[...] = jnp.zeros_like(from_x)

    @pl.when(jnp.logical_not(before_y))
    def _():
        from_y[...] = jnp.zeros_like(from_y)
        halo_from_y[...] = jnp.zeros_like(halo_from_y)

    @pl.when(jnp.logical_not(after_y))
    def _():
        for ref in (from_after, halo_from_after, vext_far, vext_corner):
            ref[...] = jnp.zeros_like(ref)

    def clear(slot, carry):
        for plane in range(EDGE + 3):
            padded[slot, pl.ds(stride * plane, rows_y), :] = jnp.zeros((rows_y, depth), F32)
        for plane in (0, EDGE + 1):
            padded[slot, pl.ds(stride * plane + rows_y, EDGE), :] = jnp.zeros((EDGE, depth), F32)
        return carry

    lax.fori_loop(0, slots, clear, 0)

    load_off_rows.wait()
    begin_x = jnp.clip(off_rows[0:1, :] - gx * rows_x, 0, rows_x - 1)
    begin_y = jnp.clip(off_rows[1:2, :] - yz * rows_y, 0, rows_y - 1)
    plane = jnp.clip(iota((rows_x + EDGE, slots), 0) - begin_x + 1, 0, EDGE + 1)
    start_rows[:, :slots] = plane * stride + rows_y - begin_y
    table = pltpu.make_async_copy(start_rows, starts, table_sem)
    table.start()

    load_syn.wait()
    syn = syn_ref[...]
    lane = iota((EDGE, CUBE), 1)
    row = iota((EDGE, CUBE), 0)
    by_i = lax.dot(syn, (lane % EDGE == row).astype(F32), precision=HIGHEST, preferred_element_type=F32)
    by_j = lax.dot(syn, (lane // EDGE == row).astype(F32), precision=HIGHEST, preferred_element_type=F32)
    for a in range(EDGE):
        high, low = split(by_i[a : a + 1, :] * by_j)
        kron_hi[a * EDGE : (a + 1) * EDGE, :] = high
        kron_lo[a * EDGE : (a + 1) * EDGE, :] = low

    load_off.wait()
    load_occ.wait()
    shift = iota((EDGE, depth), 1) - iota((EDGE, depth), 0)
    places = jnp.concatenate([(shift == off[2, f]).astype(F32) for f in range(slots)], axis=1)
    placed = lax.dot_general(syn, places, (((0,), (0,)), ((), ())), precision=HIGHEST, preferred_element_type=F32)
    placed_hi, placed_lo = split(placed)
    nothing = jnp.zeros((EDGE, depth), BF16)
    for pair in range(pairs):
        for piece, source in enumerate((placed_hi, placed_hi, placed_lo)):
            for h in range(PAIR):
                f = pair * PAIR + h
                at = (piece * PAIR + h) * EDGE
                for lanes in range(PAIR):
                    what = source[:, f * depth : (f + 1) * depth] if lanes == h else nothing
                    filt[pair, at : at + EDGE, lanes * depth : (lanes + 1) * depth] = what

    def corner(f):
        x = jnp.clip(off[0, f] - gx * rows_x, 0, rows_x - 1)
        y = jnp.clip(off[1, f] - yz * rows_y, 0, rows_y - 1)
        return x, y

    load_coef.wait()
    swapped[...] = swap_in_blocks(coef[...].reshape(slots * EDGE, CUBE).astype(F32)).astype(BF16)

    span = PAIR * EDGE

    def synthesize(pair, carry):
        part = swapped[pl.ds(pl.multiple_of(pair * span, span), span), :]
        part = jnp.concatenate([part, part, part], axis=0)
        inner = dot_nt(kron_hi[...], part) + dot_nt(kron_lo[...], part)
        high = inner.astype(BF16).astype(F32)
        where = iota(inner.shape, 1)
        packed = jnp.where((where >= span) & (where < 2 * span), inner - high, high).astype(BF16)
        values = dot(packed, filt[pair])
        for h in range(PAIR):
            f = pair * PAIR + h
            value = values[:, h * depth : (h + 1) * depth]
            psi[f] = value
            weight = jnp.where(f < live[0], occ[f], 0.0)
            square = value * value * weight
            for a in range(EDGE):
                padded[f, pl.ds(stride * (a + 1) + rows_y, EDGE), :] = square[a * EDGE : (a + 1) * EDGE, :]
        return carry

    issued = []

    def copy(there, src, dst, device, arrives):
        index = len(issued)
        descriptor = pltpu.make_async_remote_copy(
            src_ref=src, dst_ref=dst, send_sem=send_sems.at[index], recv_sem=recv_sems.at[index],
            device_id=device, device_id_type=MESH,
        )

        @pl.when(there)
        def _():
            descriptor.start()

        issued.append((there, descriptor))

        def landed():
            @pl.when(arrives)
            def _():
                descriptor.wait_recv()

        return landed

    groups = REACH // GROUP
    rest = rows_x - REACH
    edge, inner, far = pl.ds(0, EDGE), pl.ds(EDGE, rows_y - EDGE), pl.ds(rows_y, EDGE)
    spans = [pl.ds(g * GROUP, GROUP) for g in range(groups)]
    beyond = [pl.ds(rows_x + g * GROUP, GROUP) for g in range(groups)]
    others = pl.ds(REACH, rest)

    pl.semaphore_wait(barrier, neighbours)
    first = pl.ds(0, REACH)
    vext_in = copy(before_y, vext_hbm.at[first, edge], vext_far, last_y, after_y)
    vext_next_in = copy(feeds, vext_hbm.at[first, edge], vext_next, last_x, alone)

    lax.fori_loop(0, pairs, synthesize, 0)

    def sum_planes(first, count, unit, own):
        def body(step, carry):
            x = first + step * unit
            totals = [None] * unit
            for f in range(slots):
                for n in range(unit):
                    rows = padded[f, pl.ds(starts[x + n, f], wide_y), :]
                    totals[n] = rows if f == 0 else totals[n] + rows
            for n in range(unit):
                if own:
                    partial[x + n, :rows_y, :] = totals[n][:rows_y] + core[x + n]
                    partial[x + n, rows_y:, :] = totals[n][rows_y:]
                else:
                    partial[x + n] = totals[n]
            return carry

        lax.fori_loop(0, count // unit, body, 0)

    table.wait()

    load_core.wait()
    sum_planes(REACH, rest, 3, True)
    rest_in = copy(after_y, partial.at[others, far], from_y.at[others], next_y, before_y)
    far_in, edge_in, inner_in, next_in = [], [], [], []
    for g in range(groups):
        sum_planes(rows_x + g * GROUP, GROUP, GROUP, False)
        far_in.append(copy(after_x, partial.at[beyond[g], far], from_x.at[spans[g], far], next_x, before_x))
        edge_in.append(copy(after_x, partial.at[beyond[g], edge], from_x.at[spans[g], edge], next_x, before_x))
        sum_planes(g * GROUP, GROUP, GROUP, True)
        for rows in (far, edge):
            next_in.append(copy(feeds, partial.at[spans[g], rows], from_next.at[spans[g], rows], last_x, alone))
    for g in range(groups):
        inner_in.append(copy(after_x, partial.at[beyond[g], inner], from_x.at[spans[g], inner], next_x, before_x))

    onward_in, back_in, halo_onward_in, halo_back_in = [], [], [], []
    for g in range(groups):
        far_in[g]()
        side_far[spans[g]] = partial[spans[g], far, :] + from_x[spans[g], far, :]
        onward_in.append(copy(after_y, side_far.at[spans[g]], from_y.at[spans[g]], next_y, before_y))
        edge_in[g]()
        side_edge[spans[g]] = partial[spans[g], edge, :] + from_x[spans[g], edge, :]
        back_in.append(copy(before_y, side_edge.at[spans[g]], from_after.at[spans[g]], last_y, after_y))
    vext_in()
    vext_corner_in = copy(feeds & after_y, vext_far, vext_corner, last_x, alone & after_y)
    def potential(planes, rows, external, *densities):
        density = functools.reduce(jnp.add, densities)
        ext[planes, rows, :] = external + XC_COEF * jnp.exp2(jnp.log2(density) * (1.0 / 3.0))

    load_vext.wait()
    waits = []
    for g in range(groups):
        inner_in[g]()
        potential(spans[g], inner, vext[spans[g], inner, :], partial[spans[g], inner, :], from_x[spans[g], inner, :])
        waits.append(copy(before_x, ext.at[spans[g], inner], ext.at[beyond[g], inner], last_x, after_x))
    rest_in()
    potential(others, edge, vext[others, edge, :], partial[others, edge, :], from_y[others])
    waits.append(copy(before_y, ext.at[others, edge], ext.at[others, far], last_y, after_y))
    potential(others, inner, vext[others, inner, :], partial[others, inner, :])
    for g in range(groups):
        next_in[2 * g]()
        next_in[2 * g + 1]()

        @pl.when(alone)
        def _(g=g):
            halo_far[spans[g]] = partial[beyond[g], far, :] + from_next[spans[g], far, :]
            halo_edge[spans[g]] = partial[beyond[g], edge, :] + from_next[spans[g], edge, :]

        halo_onward_in.append(copy(
            alone & after_y, halo_far.at[spans[g]], halo_from_y.at[spans[g]], next_y, alone & before_y))
        halo_back_in.append(copy(
            alone & before_y, halo_edge.at[spans[g]], halo_from_after.at[spans[g]], last_y, alone & after_y))
        onward_in[g]()
        potential(spans[g], edge, vext[spans[g], edge, :], side_edge[spans[g]], from_y[spans[g]])
        waits.append(copy(odd, ext.at[spans[g], edge], ext.at[beyond[g], edge], last_x, takes))
        back_in[g]()
        potential(spans[g], far, vext_far[spans[g]], side_far[spans[g]], from_after[spans[g]])
        waits.append(copy(odd, ext.at[spans[g], far], ext.at[beyond[g], far], last_x, takes))
    vext_next_in()
    vext_corner_in()
    for g in range(groups):
        halo_onward_in[g]()
        halo_back_in[g]()

        @pl.when(alone)
        def _(g=g):
            potential(beyond[g], edge, vext_next[spans[g]], halo_edge[spans[g]], halo_from_y[spans[g]])
            potential(beyond[g], far, vext_corner[spans[g]], halo_far[spans[g]], halo_from_after[spans[g]])

    for landed in waits:
        landed()

    def analyze(pair, carry):
        parts = []
        for h in range(PAIR):
            f = pair * PAIR + h
            x, y = corner(f)
            box = ext[pl.ds(x, EDGE), pl.ds(y, EDGE), :].reshape(CUBE, depth)
            parts.append(box * psi[f])
        high, low = split(jnp.concatenate(parts, axis=1))
        left = filt[pair]
        both = dot_nt(left[span:], high)
        inner = both[:span] + both[span:] + dot_nt(left[:span], low)
        back[pl.ds(pl.multiple_of(pair * span, span), span), :] = inner
        return carry

    lax.fori_loop(0, pairs, analyze, 0)
    high, low = split(back[...])
    result = dot(high, kron_hi[...]) + (dot(high, kron_lo[...]) + dot(low, kron_hi[...]))
    result = swap_in_blocks(result)
    used = iota(result.shape, 0) < live[0] * EDGE
    result = jnp.where(used, result, 0.0)
    hpsi_ref[...] = result.astype(BF16).reshape(slots, EDGE, CUBE)

    for there, descriptor in issued:
        @pl.when(there)
        def _(descriptor=descriptor):
            descriptor.wait_send()


def deliver(hpsi_ref, ext, hpsi_hbm, pot_hbm, sems):
    rows_x, rows_y, _ = pot_hbm.shape
    copies = (
        pltpu.make_async_copy(hpsi_ref, hpsi_hbm, sems.at[0]),
        pltpu.make_async_copy(ext.at[pl.ds(0, rows_x), pl.ds(0, rows_y)], pot_hbm, sems.at[1]),
    )
    for copy in copies:
        copy.start()
    for copy in copies:
        copy.wait()


def shards(n_gx, n_yz, coeffs, occupation, box_offset, live_count, synthesis, v_ext, core_density):
    slots = coeffs.shape[0]
    rows_x, rows_y, depth = v_ext.shape
    wide_x, wide_y = rows_x + EDGE, rows_y + EDGE
    exchanges = 5 + 12 * (REACH // GROUP)
    vmem = pl.BlockSpec(memory_space=pltpu.VMEM)
    hbm = pl.BlockSpec(memory_space=pltpu.HBM)
    inputs = (occupation, box_offset.T, live_count, synthesis, coeffs, v_ext, core_density)
    hpsi, ext = pl.pallas_call(
        functools.partial(kernel, (slots, rows_x, rows_y, depth, n_gx, n_yz)),
        out_shape=(pltpu.VMEM(coeffs.shape, BF16), pltpu.VMEM((wide_x, wide_y, depth), F32)),
        in_specs=[hbm, hbm, pl.BlockSpec(memory_space=pltpu.SMEM), hbm, hbm, hbm, hbm],
        out_specs=(vmem, vmem),
        scratch_shapes=[
            pltpu.SMEM(occupation.shape, F32),
            pltpu.SMEM((3, slots), jnp.int32),
            pltpu.VMEM((3, slots), jnp.int32),
            pltpu.VMEM(synthesis.shape, F32),
            pltpu.VMEM(coeffs.shape, BF16),
            pltpu.VMEM(v_ext.shape, F32),
            pltpu.VMEM(v_ext.shape, F32),
            pltpu.VMEM((wide_x, 128), jnp.int32),
            pltpu.SMEM((wide_x, 128), jnp.int32),
            pltpu.VMEM((slots * EDGE, CUBE), BF16),
            pltpu.VMEM((CUBE, CUBE), BF16),
            pltpu.VMEM((CUBE, CUBE), BF16),
            pltpu.VMEM((slots // PAIR, 3 * PAIR * EDGE, PAIR * depth), BF16),
            pltpu.VMEM((slots, CUBE, depth), F32),
            pltpu.VMEM((slots, wide_y * (EDGE + 2) + rows_y, depth), F32),
            pltpu.VMEM((wide_x, wide_y, depth), F32),
            pltpu.VMEM((REACH, wide_y, depth), F32),
            pltpu.VMEM((rows_x, EDGE, depth), F32),
            pltpu.VMEM((REACH, EDGE, depth), F32),
            pltpu.VMEM((REACH, EDGE, depth), F32),
            pltpu.VMEM((REACH, wide_y, depth), F32),
            *[pltpu.VMEM((REACH, EDGE, depth), F32)] * 8,
            pltpu.VMEM((slots * EDGE, CUBE), F32),
            pltpu.SemaphoreType.DMA((len(inputs),)),
            pltpu.SemaphoreType.DMA,
            pltpu.SemaphoreType.DMA((exchanges,)),
            pltpu.SemaphoreType.DMA((exchanges,)),
        ],
        compiler_params=pltpu.CompilerParams(
            collective_id=0, has_side_effects=True, vmem_limit_bytes=40 * 1024 * 1024
        ),
    )(*(v if v is live_count else pltpu.with_memory_space_constraint(v, pltpu.HBM) for v in inputs))
    return pl.pallas_call(
        deliver,
        out_shape=(jax.ShapeDtypeStruct(coeffs.shape, BF16), jax.ShapeDtypeStruct(v_ext.shape, F32)),
        in_specs=[vmem, vmem],
        out_specs=(hbm, hbm),
        scratch_shapes=[pltpu.SemaphoreType.DMA((2,))],
        compiler_params=pltpu.CompilerParams(vmem_limit_bytes=16 * 1024 * 1024),
    )(hpsi, ext)


def solution(mesh):
    placed = (
        P(("gx", "yz"), None, None),
        P(("gx", "yz")),
        P(("gx", "yz"), None),
        P(("gx", "yz")),
        P(),
        P("gx", "yz", None),
        P("gx", "yz", None),
    )
    return jax.shard_map(
        functools.partial(shards, mesh.shape["gx"], mesh.shape["yz"]),
        mesh=mesh,
        in_specs=placed,
        out_specs=(P(("gx", "yz"), None, None), P("gx", "yz", None)),
        check_vma=False,
    )
```

```python
import functools

import jax
import jax.numpy as jnp
from jax import lax
from jax.experimental import pallas as pl
from jax.experimental.pallas import tpu as pltpu
from jax.sharding import PartitionSpec as P

XC_COEF = -0.9847450218426964
EDGE = 16
CUBE = EDGE * EDGE
REACH = EDGE - 1
CHUNK = 4
GROUP = 5
F32 = jnp.float32
BF16 = jnp.bfloat16
HIGHEST = lax.Precision.HIGHEST
MESH = pl.DeviceIdType.MESH


def iota(shape, dim):
    return lax.broadcasted_iota(jnp.int32, shape, dim)


def split(value):
    high = value.astype(BF16)
    low = (value - high.astype(F32)).astype(BF16)
    return high, low


def dot(left, right):
    return lax.dot_general(left, right, (((1,), (0,)), ((), ())), preferred_element_type=F32)


def swap_blocks(value):
    half = EDGE // 2
    tiles = [
        [[value[p * EDGE : (p + 1) * EDGE, t * 128 : (t + 1) * 128] for p in range(u * half, (u + 1) * half)] for t in range(2)]
        for u in range(2)
    ]
    block = iota((EDGE, 128), 1) // EDGE
    rows = []
    for u in range(2):
        parts = []
        for t in range(2):
            part = tiles[t][u]
            for step in (1, 2, 4):
                there = (block & step) != 0
                part = [
                    jnp.where(there, part[p], pltpu.roll(part[p - step], 128 - step * EDGE, 1))
                    if p & step
                    else jnp.where(there, pltpu.roll(part[p + step], step * EDGE, 1), part[p])
                    for p in range(half)
                ]
            parts.append(jnp.concatenate(part, axis=0))
        rows.append(jnp.concatenate(parts, axis=1))
    return jnp.concatenate(rows, axis=0)


def kernel(
    sizes,
    occ_hbm, off_hbm, live, syn_hbm, coef_hbm, vext_hbm, core_hbm,
    hpsi_ref, ext,
    occ, off, off_rows, syn_ref, coef, vext, core, start_rows, starts,
    kron, back, filt, taps, psi, square, boxes, padded, partial, from_x, from_y, from_after, vext_far,
    from_next, vext_next, vext_corner, side_far, side_edge, halo_far, halo_edge, halo_from_y, halo_from_after,
    in_sems, table_sem, send_sems, recv_sems,
):
    slots, rows_x, rows_y, depth, n_gx, n_yz = sizes
    gx, yz = lax.axis_index("gx"), lax.axis_index("yz")
    wide_y = rows_y + EDGE
    stride = wide_y
    per_half = depth // EDGE

    inputs = (
        (coef_hbm, coef), (off_hbm, off), (off_hbm, off_rows), (syn_hbm, syn_ref), (occ_hbm, occ),
        (core_hbm, core), (vext_hbm, vext),
    )
    loads = [pltpu.make_async_copy(src, dst, in_sems.at[n]) for n, (src, dst) in enumerate(inputs)]
    for load in loads:
        load.start()
    load_coef, load_off, load_off_rows, load_syn, load_occ, load_core, load_vext = loads

    after_x, before_x = gx < n_gx - 1, gx > 0
    after_y, before_y = yz < n_yz - 1, yz > 0
    next_x, next_y, last_x, last_y = (gx + 1, yz), (gx, yz + 1), (gx - 1, yz), (gx, yz - 1)
    odd = lax.rem(gx, 2) == 1
    even = jnp.logical_not(odd)
    alone, feeds, takes = odd & after_x, even & before_x, even & after_x
    barrier = pltpu.get_barrier_semaphore()
    neighbours = 0
    for there, device in ((after_x, next_x), (after_y, next_y), (before_x, last_x), (before_y, last_y)):
        @pl.when(there)
        def _(device=device):
            pl.semaphore_signal(barrier, inc=1, device_id=device, device_id_type=MESH)

        neighbours = neighbours + there.astype(jnp.int32)

    @pl.when(jnp.logical_not(before_x))
    def _():
        from_x[...] = jnp.zeros_like(from_x)

    @pl.when(jnp.logical_not(before_y))
    def _():
        from_y[...] = jnp.zeros_like(from_y)
        halo_from_y[...] = jnp.zeros_like(halo_from_y)

    @pl.when(jnp.logical_not(after_y))
    def _():
        for ref in (from_after, halo_from_after, vext_far, vext_corner):
            ref[...] = jnp.zeros_like(ref)

    def clear(slot, carry):
        for plane in range(EDGE + 3):
            padded[slot, pl.ds(stride * plane, rows_y), :] = jnp.zeros((rows_y, depth), F32)
        for plane in (0, EDGE + 1):
            padded[slot, pl.ds(stride * plane + rows_y, EDGE), :] = jnp.zeros((EDGE, depth), F32)
        return carry

    lax.fori_loop(0, slots, clear, 0)

    load_off_rows.wait()
    begin_x = jnp.clip(off_rows[0:1, :] - gx * rows_x, 0, rows_x - 1)
    begin_y = jnp.clip(off_rows[1:2, :] - yz * rows_y, 0, rows_y - 1)
    plane = jnp.clip(iota((rows_x + EDGE, slots), 0) - begin_x + 1, 0, EDGE + 1)
    start_rows[:, :slots] = plane * stride + rows_y - begin_y
    table = pltpu.make_async_copy(start_rows, starts, table_sem)
    table.start()

    load_syn.wait()
    syn = syn_ref[...]
    lane = iota((EDGE, CUBE), 1)
    row = iota((EDGE, CUBE), 0)
    inside, outside = (lane % EDGE == row).astype(F32), (lane // EDGE == row).astype(F32)

    def exact(contract, right):
        return lax.dot_general(
            syn, right, (((contract,), (0,)), ((), ())), precision=HIGHEST, preferred_element_type=F32)

    by_i, by_j, by_a, by_b = exact(1, inside), exact(1, outside), exact(0, outside), exact(0, inside)
    for n in range(EDGE):
        rows = slice(n * EDGE, (n + 1) * EDGE)
        here = lane // EDGE == n
        for refs, value in (
            (kron, by_i[n : n + 1, :] * by_j),
            (back, by_b[n : n + 1, :] * by_a),
            (filt, jnp.where(here, by_b, 0.0)),
            (taps, jnp.where(here, by_i, 0.0)),
        ):
            high, low = split(value)
            refs[0, rows, :] = high
            refs[1, rows, :] = low

    def corner(f):
        x = jnp.clip(off[0, f] - gx * rows_x, 0, rows_x - 1)
        y = jnp.clip(off[1, f] - yz * rows_y, 0, rows_y - 1)
        return x, y

    load_off.wait()
    load_occ.wait()
    load_coef.wait()
    swapped = swap_blocks(coef[...].reshape(slots * EDGE, CUBE).astype(F32)).astype(BF16)
    inner_high, inner_low = split(dot(kron[0], swapped) + dot(kron[1], swapped))
    psi[...] = dot(inner_high, filt[0]) + (dot(inner_low, filt[0]) + dot(inner_high, filt[1]))

    owner = iota((1, CUBE), 1) // EDGE
    weights = jnp.zeros((1, CUBE), F32)
    for f in range(slots):
        weights = jnp.where(owner == f, jnp.where(f < live[0], occ[f], 0.0), weights)
    square[...] = psi[...] * psi[...] * weights

    def place(n, carry):
        for half in range(CUBE // depth):
            f = half * per_half + n
            z = off[2, f]
            value = pltpu.roll(square[:, half * depth : (half + 1) * depth], lax.rem(z - n * EDGE + depth, depth), 1)
            along = iota((1, depth), 1) - z
            value = jnp.where((along >= 0) & (along < EDGE), value, 0.0)
            for a in range(EDGE):
                padded[f, pl.ds(stride * (a + 1) + rows_y, EDGE), :] = value[a * EDGE : (a + 1) * EDGE, :]
        return carry

    issued = []

    def copy(there, src, dst, device, arrives):
        index = len(issued)
        descriptor = pltpu.make_async_remote_copy(
            src_ref=src, dst_ref=dst, send_sem=send_sems.at[index], recv_sem=recv_sems.at[index],
            device_id=device, device_id_type=MESH,
        )

        @pl.when(there)
        def _():
            descriptor.start()

        issued.append((there, descriptor))

        def landed():
            @pl.when(arrives)
            def _():
                descriptor.wait_recv()

        return landed

    groups = REACH // GROUP
    rest = rows_x - REACH
    edge, inner, far = pl.ds(0, EDGE), pl.ds(EDGE, rows_y - EDGE), pl.ds(rows_y, EDGE)
    spans = [pl.ds(g * GROUP, GROUP) for g in range(groups)]
    beyond = [pl.ds(rows_x + g * GROUP, GROUP) for g in range(groups)]
    others = pl.ds(REACH, rest)

    pl.semaphore_wait(barrier, neighbours)
    first = pl.ds(0, REACH)
    vext_in = copy(before_y, vext_hbm.at[first, edge], vext_far, last_y, after_y)
    vext_next_in = copy(feeds, vext_hbm.at[first, edge], vext_next, last_x, alone)

    lax.fori_loop(0, per_half, place, 0)

    def sum_planes(first, count, unit, own):
        def body(step, carry):
            x = first + step * unit
            totals = [None] * unit
            for f in range(slots):
                for n in range(unit):
                    rows = padded[f, pl.ds(starts[x + n, f], wide_y), :]
                    totals[n] = rows if f == 0 else totals[n] + rows
            for n in range(unit):
                if own:
                    partial[x + n, :rows_y, :] = totals[n][:rows_y] + core[x + n]
                    partial[x + n, rows_y:, :] = totals[n][rows_y:]
                else:
                    partial[x + n] = totals[n]
            return carry

        lax.fori_loop(0, count // unit, body, 0)

    table.wait()

    load_core.wait()
    sum_planes(REACH, rest, 3, True)
    rest_in = copy(after_y, partial.at[others, far], from_y.at[others], next_y, before_y)
    far_in, edge_in, inner_in, next_in = [], [], [], []
    for g in range(groups):
        sum_planes(rows_x + g * GROUP, GROUP, GROUP, False)
        far_in.append(copy(after_x, partial.at[beyond[g], far], from_x.at[spans[g], far], next_x, before_x))
        edge_in.append(copy(after_x, partial.at[beyond[g], edge], from_x.at[spans[g], edge], next_x, before_x))
        sum_planes(g * GROUP, GROUP, GROUP, True)
        for rows in (far, edge):
            next_in.append(copy(feeds, partial.at[spans[g], rows], from_next.at[spans[g], rows], last_x, alone))
    for g in range(groups):
        inner_in.append(copy(after_x, partial.at[beyond[g], inner], from_x.at[spans[g], inner], next_x, before_x))

    onward_in, back_in, halo_onward_in, halo_back_in = [], [], [], []
    for g in range(groups):
        far_in[g]()
        side_far[spans[g]] = partial[spans[g], far, :] + from_x[spans[g], far, :]
        onward_in.append(copy(after_y, side_far.at[spans[g]], from_y.at[spans[g]], next_y, before_y))
        edge_in[g]()
        side_edge[spans[g]] = partial[spans[g], edge, :] + from_x[spans[g], edge, :]
        back_in.append(copy(before_y, side_edge.at[spans[g]], from_after.at[spans[g]], last_y, after_y))
    vext_in()
    vext_corner_in = copy(feeds & after_y, vext_far, vext_corner, last_x, alone & after_y)
    def potential(planes, rows, external, *densities):
        density = functools.reduce(jnp.add, densities)
        ext[planes, rows, :] = external + XC_COEF * jnp.exp2(jnp.log2(density) * (1.0 / 3.0))

    load_vext.wait()
    waits = []
    for g in range(groups):
        inner_in[g]()
        potential(spans[g], inner, vext[spans[g], inner, :], partial[spans[g], inner, :], from_x[spans[g], inner, :])
        waits.append(copy(before_x, ext.at[spans[g], inner], ext.at[beyond[g], inner], last_x, after_x))
    rest_in()
    potential(others, edge, vext[others, edge, :], partial[others, edge, :], from_y[others])
    waits.append(copy(before_y, ext.at[others, edge], ext.at[others, far], last_y, after_y))
    potential(others, inner, vext[others, inner, :], partial[others, inner, :])
    for g in range(groups):
        next_in[2 * g]()
        next_in[2 * g + 1]()

        @pl.when(alone)
        def _(g=g):
            halo_far[spans[g]] = partial[beyond[g], far, :] + from_next[spans[g], far, :]
            halo_edge[spans[g]] = partial[beyond[g], edge, :] + from_next[spans[g], edge, :]

        halo_onward_in.append(copy(
            alone & after_y, halo_far.at[spans[g]], halo_from_y.at[spans[g]], next_y, alone & before_y))
        halo_back_in.append(copy(
            alone & before_y, halo_edge.at[spans[g]], halo_from_after.at[spans[g]], last_y, alone & after_y))
        onward_in[g]()
        potential(spans[g], edge, vext[spans[g], edge, :], side_edge[spans[g]], from_y[spans[g]])
        waits.append(copy(odd, ext.at[spans[g], edge], ext.at[beyond[g], edge], last_x, takes))
        back_in[g]()
        potential(spans[g], far, vext_far[spans[g]], side_far[spans[g]], from_after[spans[g]])
        waits.append(copy(odd, ext.at[spans[g], far], ext.at[beyond[g], far], last_x, takes))
    vext_next_in()
    vext_corner_in()
    for g in range(groups):
        halo_onward_in[g]()
        halo_back_in[g]()

        @pl.when(alone)
        def _(g=g):
            potential(beyond[g], edge, vext_next[spans[g]], halo_edge[spans[g]], halo_from_y[spans[g]])
            potential(beyond[g], far, vext_corner[spans[g]], halo_far[spans[g]], halo_from_after[spans[g]])

    for landed in waits:
        landed()

    def collect(part, carry):
        rows = pl.ds(pl.multiple_of(part * CHUNK * EDGE, CHUNK * EDGE), CHUNK * EDGE)
        block = iota((1, depth), 1) // EDGE
        for half in range(CUBE // depth):
            total = None
            for n in range(per_half):
                f = half * per_half + n
                x, y = corner(f)
                box = ext[pl.ds(x + part * CHUNK, CHUNK), pl.ds(y, EDGE), :].reshape(CHUNK * EDGE, depth)
                box = pltpu.roll(box, lax.rem(n * EDGE - off[2, f] + depth, depth), 1)
                total = box if n == 0 else jnp.where(block == n, box, total)
            boxes[rows, half * depth : (half + 1) * depth] = total
        return carry

    lax.fori_loop(0, EDGE // CHUNK, collect, 0)
    high, low = split(boxes[...] * psi[...])
    high, low = split(dot(high, taps[0]) + (dot(high, taps[1]) + dot(low, taps[0])))
    result = dot(back[0], high) + (dot(back[0], low) + dot(back[1], high))
    result = swap_blocks(result)
    used = iota(result.shape, 0) < live[0] * EDGE
    result = jnp.where(used, result, 0.0)
    hpsi_ref[...] = result.astype(BF16).reshape(slots, EDGE, CUBE)

    for there, descriptor in issued:
        @pl.when(there)
        def _(descriptor=descriptor):
            descriptor.wait_send()


def deliver(hpsi_ref, ext, hpsi_hbm, pot_hbm, sems):
    rows_x, rows_y, _ = pot_hbm.shape
    copies = (
        pltpu.make_async_copy(hpsi_ref, hpsi_hbm, sems.at[0]),
        pltpu.make_async_copy(ext.at[pl.ds(0, rows_x), pl.ds(0, rows_y)], pot_hbm, sems.at[1]),
    )
    for copy in copies:
        copy.start()
    for copy in copies:
        copy.wait()


def shards(n_gx, n_yz, coeffs, occupation, box_offset, live_count, synthesis, v_ext, core_density):
    slots = coeffs.shape[0]
    rows_x, rows_y, depth = v_ext.shape
    wide_x, wide_y = rows_x + EDGE, rows_y + EDGE
    exchanges = 5 + 12 * (REACH // GROUP)
    vmem = pl.BlockSpec(memory_space=pltpu.VMEM)
    hbm = pl.BlockSpec(memory_space=pltpu.HBM)
    inputs = (occupation, box_offset.T, live_count, synthesis, coeffs, v_ext, core_density)
    hpsi, ext = pl.pallas_call(
        functools.partial(kernel, (slots, rows_x, rows_y, depth, n_gx, n_yz)),
        out_shape=(pltpu.VMEM(coeffs.shape, BF16), pltpu.VMEM((wide_x, wide_y, depth), F32)),
        in_specs=[hbm, hbm, pl.BlockSpec(memory_space=pltpu.SMEM), hbm, hbm, hbm, hbm],
        out_specs=(vmem, vmem),
        scratch_shapes=[
            pltpu.SMEM(occupation.shape, F32),
            pltpu.SMEM((3, slots), jnp.int32),
            pltpu.VMEM((3, slots), jnp.int32),
            pltpu.VMEM(synthesis.shape, F32),
            pltpu.VMEM(coeffs.shape, BF16),
            pltpu.VMEM(v_ext.shape, F32),
            pltpu.VMEM(v_ext.shape, F32),
            pltpu.VMEM((wide_x, 128), jnp.int32),
            pltpu.SMEM((wide_x, 128), jnp.int32),
            *[pltpu.VMEM((2, CUBE, CUBE), BF16)] * 4,
            *[pltpu.VMEM((CUBE, CUBE), F32)] * 3,
            pltpu.VMEM((slots, wide_y * (EDGE + 2) + rows_y, depth), F32),
            pltpu.VMEM((wide_x, wide_y, depth), F32),
            pltpu.VMEM((REACH, wide_y, depth), F32),
            pltpu.VMEM((rows_x, EDGE, depth), F32),
            pltpu.VMEM((REACH, EDGE, depth), F32),
            pltpu.VMEM((REACH, EDGE, depth), F32),
            pltpu.VMEM((REACH, wide_y, depth), F32),
            *[pltpu.VMEM((REACH, EDGE, depth), F32)] * 8,
            pltpu.SemaphoreType.DMA((len(inputs),)),
            pltpu.SemaphoreType.DMA,
            pltpu.SemaphoreType.DMA((exchanges,)),
            pltpu.SemaphoreType.DMA((exchanges,)),
        ],
        compiler_params=pltpu.CompilerParams(
            collective_id=0, has_side_effects=True, vmem_limit_bytes=40 * 1024 * 1024
        ),
    )(*(v if v is live_count else pltpu.with_memory_space_constraint(v, pltpu.HBM) for v in inputs))
    return pl.pallas_call(
        deliver,
        out_shape=(jax.ShapeDtypeStruct(coeffs.shape, BF16), jax.ShapeDtypeStruct(v_ext.shape, F32)),
        in_specs=[vmem, vmem],
        out_specs=(hbm, hbm),
        scratch_shapes=[pltpu.SemaphoreType.DMA((2,))],
        compiler_params=pltpu.CompilerParams(vmem_limit_bytes=16 * 1024 * 1024),
    )(hpsi, ext)


def solution(mesh):
    placed = (
        P(("gx", "yz"), None, None),
        P(("gx", "yz")),
        P(("gx", "yz"), None),
        P(("gx", "yz")),
        P(),
        P("gx", "yz", None),
        P("gx", "yz", None),
    )
    return jax.shard_map(
        functools.partial(shards, mesh.shape["gx"], mesh.shape["yz"]),
        mesh=mesh,
        in_specs=placed,
        out_specs=(P(("gx", "yz"), None, None), P("gx", "yz", None)),
        check_vma=False,
    )
```

```python
import functools

import jax
import jax.numpy as jnp
from jax import lax
from jax.experimental import pallas as pl
from jax.experimental.pallas import tpu as pltpu
from jax.sharding import PartitionSpec as P

XC_COEF = -0.9847450218426964
EDGE = 16
CUBE = EDGE * EDGE
REACH = EDGE - 1
CHUNK = 4
GROUP = 5
F32 = jnp.float32
BF16 = jnp.bfloat16
HIGHEST = lax.Precision.HIGHEST
MESH = pl.DeviceIdType.MESH


def iota(shape, dim):
    return lax.broadcasted_iota(jnp.int32, shape, dim)


def split(value):
    high = value.astype(BF16)
    low = (value - high.astype(F32)).astype(BF16)
    return high, low


def dot(left, right):
    return lax.dot_general(left, right, (((1,), (0,)), ((), ())), preferred_element_type=F32)


def swap_blocks(value):
    half = EDGE // 2
    tiles = [
        [[value[p * EDGE : (p + 1) * EDGE, t * 128 : (t + 1) * 128] for p in range(u * half, (u + 1) * half)] for t in range(2)]
        for u in range(2)
    ]
    block = iota((EDGE, 128), 1) // EDGE
    rows = []
    for u in range(2):
        parts = []
        for t in range(2):
            part = tiles[t][u]
            for step in (1, 2, 4):
                there = (block & step) != 0
                part = [
                    jnp.where(there, part[p], pltpu.roll(part[p - step], 128 - step * EDGE, 1))
                    if p & step
                    else jnp.where(there, pltpu.roll(part[p + step], step * EDGE, 1), part[p])
                    for p in range(half)
                ]
            parts.append(jnp.concatenate(part, axis=0))
        rows.append(jnp.concatenate(parts, axis=1))
    return jnp.concatenate(rows, axis=0)


def kernel(
    sizes,
    occ_hbm, off_hbm, live, syn_hbm, coef_hbm, vext_hbm, core_hbm,
    boxes, back, ext,
    occ, off_rows, syn_ref, coef, vext, core, start_rows, starts,
    kron, filt, taps, psi, square, padded, partial, from_x, from_y, from_after, vext_far,
    from_next, vext_next, vext_corner, side_far, side_edge, halo_far, halo_edge, halo_from_y, halo_from_after,
    in_sems, table_sem, send_sems, recv_sems,
):
    slots, rows_x, rows_y, depth, n_gx, n_yz = sizes
    gx, yz = lax.axis_index("gx"), lax.axis_index("yz")
    wide_y = rows_y + EDGE
    stride = wide_y
    per_half = depth // EDGE

    inputs = (
        (coef_hbm, coef), (off_hbm, off_rows), (syn_hbm, syn_ref), (occ_hbm, occ),
        (core_hbm, core), (vext_hbm, vext),
    )
    loads = [pltpu.make_async_copy(src, dst, in_sems.at[n]) for n, (src, dst) in enumerate(inputs)]
    for load in loads:
        load.start()
    load_coef, load_off_rows, load_syn, load_occ, load_core, load_vext = loads

    after_x, before_x = gx < n_gx - 1, gx > 0
    after_y, before_y = yz < n_yz - 1, yz > 0
    next_x, next_y, last_x, last_y = (gx + 1, yz), (gx, yz + 1), (gx - 1, yz), (gx, yz - 1)
    odd = lax.rem(gx, 2) == 1
    even = jnp.logical_not(odd)
    alone, feeds, takes = odd & after_x, even & before_x, even & after_x
    barrier = pltpu.get_barrier_semaphore()
    neighbours = 0
    for there, device in ((after_x, next_x), (after_y, next_y), (before_x, last_x), (before_y, last_y)):
        @pl.when(there)
        def _(device=device):
            pl.semaphore_signal(barrier, inc=1, device_id=device, device_id_type=MESH)

        neighbours = neighbours + there.astype(jnp.int32)

    @pl.when(jnp.logical_not(before_x))
    def _():
        from_x[...] = jnp.zeros_like(from_x)

    @pl.when(jnp.logical_not(before_y))
    def _():
        from_y[...] = jnp.zeros_like(from_y)
        halo_from_y[...] = jnp.zeros_like(halo_from_y)

    @pl.when(jnp.logical_not(after_y))
    def _():
        for ref in (from_after, halo_from_after, vext_far, vext_corner):
            ref[...] = jnp.zeros_like(ref)

    def clear(slot, carry):
        for plane in range(EDGE + 3):
            padded[slot, pl.ds(stride * plane, rows_y), :] = jnp.zeros((rows_y, depth), F32)
        for plane in (0, EDGE + 1):
            padded[slot, pl.ds(stride * plane + rows_y, EDGE), :] = jnp.zeros((EDGE, depth), F32)
        return carry

    lax.fori_loop(0, slots, clear, 0)

    at_x, at_y, at_z, turn_to, turn_from = (rows_x + EDGE + n for n in range(5))
    load_off_rows.wait()
    begin_x = jnp.clip(off_rows[0:1, :] - gx * rows_x, 0, rows_x - 1)
    begin_y = jnp.clip(off_rows[1:2, :] - yz * rows_y, 0, rows_y - 1)
    plane = jnp.clip(iota((rows_x + EDGE, slots), 0) - begin_x + 1, 0, EDGE + 1)
    begin_z = off_rows[2:3, :]
    turn = begin_z - (iota((1, slots), 1) % per_half) * EDGE
    start_rows[: rows_x + EDGE, :slots] = plane * stride + rows_y - begin_y
    for n, value in enumerate((begin_x, begin_y, begin_z, turn & (depth - 1), (-turn) & (depth - 1))):
        start_rows[rows_x + EDGE + n : rows_x + EDGE + n + 1, :slots] = value
    table = pltpu.make_async_copy(start_rows, starts, table_sem)
    table.start()

    load_syn.wait()
    syn = syn_ref[...]
    lane = iota((EDGE, CUBE), 1)
    row = iota((EDGE, CUBE), 0)
    inside, outside = (lane % EDGE == row).astype(F32), (lane // EDGE == row).astype(F32)

    def exact(contract, right):
        return lax.dot_general(
            syn, right, (((contract,), (0,)), ((), ())), precision=HIGHEST, preferred_element_type=F32)

    by_i, by_j, by_a, by_b = exact(1, inside), exact(1, outside), exact(0, outside), exact(0, inside)
    for n in range(EDGE):
        rows = slice(n * EDGE, (n + 1) * EDGE)
        here = lane // EDGE == n
        for refs, value in (
            (kron, by_i[n : n + 1, :] * by_j),
            (back, by_b[n : n + 1, :] * by_a),
            (filt, jnp.where(here, by_b, 0.0)),
            (taps, jnp.where(here, by_i, 0.0)),
        ):
            high, low = split(value)
            refs[0, rows, :] = high
            refs[1, rows, :] = low

    load_occ.wait()
    load_coef.wait()
    swapped = swap_blocks(coef[...].reshape(slots * EDGE, CUBE).astype(F32)).astype(BF16)
    inner_high, inner_low = split(dot(kron[0], swapped) + dot(kron[1], swapped))
    psi[...] = dot(inner_high, filt[0]) + (dot(inner_low, filt[0]) + dot(inner_high, filt[1]))

    owner = iota((1, CUBE), 1) // EDGE
    weights = jnp.zeros((1, CUBE), F32)
    for f in range(slots):
        weights = jnp.where(owner == f, jnp.where(f < live[0], occ[f], 0.0), weights)
    square[...] = psi[...] * psi[...] * weights

    def place(n, carry):
        for half in range(CUBE // depth):
            f = half * per_half + n
            value = pltpu.roll(square[:, half * depth : (half + 1) * depth], starts[turn_to, f], 1)
            along = iota((1, depth), 1) - starts[at_z, f]
            value = jnp.where((along >= 0) & (along < EDGE), value, 0.0)
            for a in range(EDGE):
                padded[f, pl.ds(stride * (a + 1) + rows_y, EDGE), :] = value[a * EDGE : (a + 1) * EDGE, :]
        return carry

    issued = []

    def copy(there, src, dst, device, arrives):
        index = len(issued)
        descriptor = pltpu.make_async_remote_copy(
            src_ref=src, dst_ref=dst, send_sem=send_sems.at[index], recv_sem=recv_sems.at[index],
            device_id=device, device_id_type=MESH,
        )

        @pl.when(there)
        def _():
            descriptor.start()

        issued.append((there, descriptor))

        def landed():
            @pl.when(arrives)
            def _():
                descriptor.wait_recv()

        return landed

    groups = REACH // GROUP
    rest = rows_x - REACH
    edge, inner, far = pl.ds(0, EDGE), pl.ds(EDGE, rows_y - EDGE), pl.ds(rows_y, EDGE)
    spans = [pl.ds(g * GROUP, GROUP) for g in range(groups)]
    beyond = [pl.ds(rows_x + g * GROUP, GROUP) for g in range(groups)]
    others = pl.ds(REACH, rest)

    pl.semaphore_wait(barrier, neighbours)
    first = pl.ds(0, REACH)
    vext_in = copy(before_y, vext_hbm.at[first, edge], vext_far, last_y, after_y)

    table.wait()
    lax.fori_loop(0, per_half, place, 0, unroll=2)

    def sum_planes(first, count, unit, own):
        def body(step, carry):
            x = first + step * unit
            totals = [None] * unit
            for f in range(slots):
                for n in range(unit):
                    rows = padded[f, pl.ds(starts[x + n, f], wide_y), :]
                    totals[n] = rows if f == 0 else totals[n] + rows
            for n in range(unit):
                if own:
                    partial[x + n, :rows_y, :] = totals[n][:rows_y] + core[x + n]
                    partial[x + n, rows_y:, :] = totals[n][rows_y:]
                else:
                    partial[x + n] = totals[n]
            return carry

        lax.fori_loop(0, count // unit, body, 0)

    load_core.wait()
    sum_planes(REACH, rest, 3, True)
    rest_in = copy(after_y, partial.at[others, far], from_y.at[others], next_y, before_y)
    far_in, edge_in, inner_in, next_in = [], [], [], []
    for g in range(groups):
        sum_planes(rows_x + g * GROUP, GROUP, GROUP, False)
        far_in.append(copy(after_x, partial.at[beyond[g], far], from_x.at[spans[g], far], next_x, before_x))
        edge_in.append(copy(after_x, partial.at[beyond[g], edge], from_x.at[spans[g], edge], next_x, before_x))
        sum_planes(g * GROUP, GROUP, GROUP, True)
        for rows in (far, edge):
            next_in.append(copy(feeds, partial.at[spans[g], rows], from_next.at[spans[g], rows], last_x, alone))
    vext_next_in = copy(feeds, vext_hbm.at[first, edge], vext_next, last_x, alone)
    for g in range(groups):
        inner_in.append(copy(after_x, partial.at[beyond[g], inner], from_x.at[spans[g], inner], next_x, before_x))

    onward_in, back_in, halo_onward_in, halo_back_in = [], [], [], []
    for g in range(groups):
        far_in[g]()
        side_far[spans[g]] = partial[spans[g], far, :] + from_x[spans[g], far, :]
        onward_in.append(copy(after_y, side_far.at[spans[g]], from_y.at[spans[g]], next_y, before_y))
        edge_in[g]()
        side_edge[spans[g]] = partial[spans[g], edge, :] + from_x[spans[g], edge, :]
        back_in.append(copy(before_y, side_edge.at[spans[g]], from_after.at[spans[g]], last_y, after_y))
    vext_in()
    vext_corner_in = copy(feeds & after_y, vext_far, vext_corner, last_x, alone & after_y)
    def potential(planes, rows, external, *densities):
        density = functools.reduce(jnp.add, densities)
        ext[planes, rows, :] = external + XC_COEF * jnp.exp2(jnp.log2(density) * (1.0 / 3.0))

    load_vext.wait()
    waits = []
    rest_in()
    potential(others, edge, vext[others, edge, :], partial[others, edge, :], from_y[others])
    waits.append(copy(before_y, ext.at[others, edge], ext.at[others, far], last_y, after_y))
    for g in range(groups):
        inner_in[g]()
        potential(spans[g], inner, vext[spans[g], inner, :], partial[spans[g], inner, :], from_x[spans[g], inner, :])
        waits.append(copy(before_x, ext.at[spans[g], inner], ext.at[beyond[g], inner], last_x, after_x))
    potential(others, inner, vext[others, inner, :], partial[others, inner, :])
    for g in range(groups):
        next_in[2 * g]()
        next_in[2 * g + 1]()

        @pl.when(alone)
        def _(g=g):
            halo_far[spans[g]] = partial[beyond[g], far, :] + from_next[spans[g], far, :]
            halo_edge[spans[g]] = partial[beyond[g], edge, :] + from_next[spans[g], edge, :]

        halo_onward_in.append(copy(
            alone & after_y, halo_far.at[spans[g]], halo_from_y.at[spans[g]], next_y, alone & before_y))
        halo_back_in.append(copy(
            alone & before_y, halo_edge.at[spans[g]], halo_from_after.at[spans[g]], last_y, alone & after_y))
        onward_in[g]()
        potential(spans[g], edge, vext[spans[g], edge, :], side_edge[spans[g]], from_y[spans[g]])
        waits.append(copy(odd, ext.at[spans[g], edge], ext.at[beyond[g], edge], last_x, takes))
        back_in[g]()
        potential(spans[g], far, vext_far[spans[g]], side_far[spans[g]], from_after[spans[g]])
        waits.append(copy(odd, ext.at[spans[g], far], ext.at[beyond[g], far], last_x, takes))
    vext_next_in()
    vext_corner_in()
    for g in range(groups):
        halo_onward_in[g]()
        halo_back_in[g]()

        @pl.when(alone)
        def _(g=g):
            potential(beyond[g], edge, vext_next[spans[g]], halo_edge[spans[g]], halo_from_y[spans[g]])
            potential(beyond[g], far, vext_corner[spans[g]], halo_far[spans[g]], halo_from_after[spans[g]])

    for landed in waits:
        landed()

    def collect(part, carry):
        rows = pl.ds(pl.multiple_of(part * CHUNK * EDGE, CHUNK * EDGE), CHUNK * EDGE)
        block = iota((1, depth), 1) // EDGE
        totals = []
        for half in range(CUBE // depth):
            total = None
            for n in range(per_half):
                f = half * per_half + n
                box = ext[pl.ds(starts[at_x, f] + part * CHUNK, CHUNK), pl.ds(starts[at_y, f], EDGE), :]
                box = pltpu.roll(box.reshape(CHUNK * EDGE, depth), starts[turn_from, f], 1)
                total = box if n == 0 else jnp.where(block == n, box, total)
            totals.append(total)
        high, low = split(jnp.concatenate(totals, axis=1) * psi[rows, :])
        value = dot(high, taps[0]) + (dot(high, taps[1]) + dot(low, taps[0]))
        high, low = split(jnp.where(iota((1, CUBE), 1) < live[0] * EDGE, value, 0.0))
        boxes[0, rows, :] = high
        boxes[1, rows, :] = low
        return carry

    lax.fori_loop(0, EDGE // CHUNK, collect, 0, unroll=4)
    for there, descriptor in issued:
        @pl.when(there)
        def _(descriptor=descriptor):
            descriptor.wait_send()


def deliver(boxes, back, ext, hpsi_hbm, pot_hbm, hpsi, sems):
    slots, _, _ = hpsi_hbm.shape
    rows_x, rows_y, _ = pot_hbm.shape
    pot_out = pltpu.make_async_copy(ext.at[pl.ds(0, rows_x), pl.ds(0, rows_y)], pot_hbm, sems.at[0])
    pot_out.start()
    high, low = boxes[0], boxes[1]
    result = dot(back[0], high) + (dot(back[0], low) + dot(back[1], high))
    hpsi[...] = swap_blocks(result).astype(BF16).reshape(slots, EDGE, CUBE)
    hpsi_out = pltpu.make_async_copy(hpsi, hpsi_hbm, sems.at[1])
    hpsi_out.start()
    pot_out.wait()
    hpsi_out.wait()


def shards(n_gx, n_yz, coeffs, occupation, box_offset, live_count, synthesis, v_ext, core_density):
    slots = coeffs.shape[0]
    rows_x, rows_y, depth = v_ext.shape
    wide_x, wide_y = rows_x + EDGE, rows_y + EDGE
    exchanges = 5 + 12 * (REACH // GROUP)
    vmem = pl.BlockSpec(memory_space=pltpu.VMEM)
    hbm = pl.BlockSpec(memory_space=pltpu.HBM)
    inputs = (occupation, box_offset.T, live_count, synthesis, coeffs, v_ext, core_density)
    boxes, back, ext = pl.pallas_call(
        functools.partial(kernel, (slots, rows_x, rows_y, depth, n_gx, n_yz)),
        out_shape=(
            pltpu.VMEM((2, CUBE, CUBE), BF16),
            pltpu.VMEM((2, CUBE, CUBE), BF16),
            pltpu.VMEM((wide_x, wide_y, depth), F32),
        ),
        in_specs=[hbm, hbm, pl.BlockSpec(memory_space=pltpu.SMEM), hbm, hbm, hbm, hbm],
        out_specs=(vmem, vmem, vmem),
        scratch_shapes=[
            pltpu.SMEM(occupation.shape, F32),
            pltpu.VMEM((3, slots), jnp.int32),
            pltpu.VMEM(synthesis.shape, F32),
            pltpu.VMEM(coeffs.shape, BF16),
            pltpu.VMEM(v_ext.shape, F32),
            pltpu.VMEM(v_ext.shape, F32),
            pltpu.VMEM((wide_x + 8, 128), jnp.int32),
            pltpu.SMEM((wide_x + 8, 128), jnp.int32),
            *[pltpu.VMEM((2, CUBE, CUBE), BF16)] * 3,
            *[pltpu.VMEM((CUBE, CUBE), F32)] * 2,
            pltpu.VMEM((slots, wide_y * (EDGE + 2) + rows_y, depth), F32),
            pltpu.VMEM((wide_x, wide_y, depth), F32),
            pltpu.VMEM((REACH, wide_y, depth), F32),
            pltpu.VMEM((rows_x, EDGE, depth), F32),
            pltpu.VMEM((REACH, EDGE, depth), F32),
            pltpu.VMEM((REACH, EDGE, depth), F32),
            pltpu.VMEM((REACH, wide_y, depth), F32),
            *[pltpu.VMEM((REACH, EDGE, depth), F32)] * 8,
            pltpu.SemaphoreType.DMA((len(inputs) - 1,)),
            pltpu.SemaphoreType.DMA,
            pltpu.SemaphoreType.DMA((exchanges,)),
            pltpu.SemaphoreType.DMA((exchanges,)),
        ],
        compiler_params=pltpu.CompilerParams(
            collective_id=0, has_side_effects=True, vmem_limit_bytes=40 * 1024 * 1024
        ),
    )(*(v if v is live_count else pltpu.with_memory_space_constraint(v, pltpu.HBM) for v in inputs))
    return pl.pallas_call(
        deliver,
        out_shape=(jax.ShapeDtypeStruct(coeffs.shape, BF16), jax.ShapeDtypeStruct(v_ext.shape, F32)),
        in_specs=[vmem, vmem, vmem],
        out_specs=(hbm, hbm),
        scratch_shapes=[pltpu.VMEM(coeffs.shape, BF16), pltpu.SemaphoreType.DMA((2,))],
        compiler_params=pltpu.CompilerParams(vmem_limit_bytes=16 * 1024 * 1024),
    )(boxes, back, ext)


def solution(mesh):
    placed = (
        P(("gx", "yz"), None, None),
        P(("gx", "yz")),
        P(("gx", "yz"), None),
        P(("gx", "yz")),
        P(),
        P("gx", "yz", None),
        P("gx", "yz", None),
    )
    return jax.shard_map(
        functools.partial(shards, mesh.shape["gx"], mesh.shape["yz"]),
        mesh=mesh,
        in_specs=placed,
        out_specs=(P(("gx", "yz"), None, None), P("gx", "yz", None)),
        check_vma=False,
    )
```

```python
import functools

import jax
import jax.numpy as jnp
from jax import lax
from jax.experimental import pallas as pl
from jax.experimental.pallas import tpu as pltpu
from jax.sharding import PartitionSpec as P

XC_COEF = -0.9847450218426964
EDGE = 16
CUBE = EDGE * EDGE
REACH = EDGE - 1
CHUNK = 4
GROUP = 5
F32 = jnp.float32
BF16 = jnp.bfloat16
HIGHEST = lax.Precision.HIGHEST
MESH = pl.DeviceIdType.MESH


def iota(shape, dim):
    return lax.broadcasted_iota(jnp.int32, shape, dim)


def split(value):
    high = value.astype(BF16)
    low = (value - high.astype(F32)).astype(BF16)
    return high, low


def dot(left, right):
    return lax.dot_general(left, right, (((1,), (0,)), ((), ())), preferred_element_type=F32)


def swap_blocks(value):
    half = EDGE // 2
    tiles = [
        [[value[p * EDGE : (p + 1) * EDGE, t * 128 : (t + 1) * 128] for p in range(u * half, (u + 1) * half)] for t in range(2)]
        for u in range(2)
    ]
    block = iota((EDGE, 128), 1) // EDGE
    rows = []
    for u in range(2):
        parts = []
        for t in range(2):
            part = tiles[t][u]
            for step in (1, 2, 4):
                there = (block & step) != 0
                part = [
                    jnp.where(there, part[p], pltpu.roll(part[p - step], 128 - step * EDGE, 1))
                    if p & step
                    else jnp.where(there, pltpu.roll(part[p + step], step * EDGE, 1), part[p])
                    for p in range(half)
                ]
            parts.append(jnp.concatenate(part, axis=0))
        rows.append(jnp.concatenate(parts, axis=1))
    return jnp.concatenate(rows, axis=0)


def kernel(
    sizes,
    occ_hbm, off_hbm, live, syn_hbm, coef_hbm, vext_hbm, core_hbm,
    boxes, back, ext,
    occ, off_rows, syn_ref, coef, vext, core, start_rows, starts,
    kron, filt, taps, psi, square, padded, partial, from_x, from_y, from_after, vext_far,
    from_next, vext_next, vext_corner, side_far, side_edge, halo_far, halo_edge, halo_from_y, halo_from_after,
    in_sems, table_sem, send_sems, recv_sems,
):
    slots, rows_x, rows_y, depth, n_gx, n_yz = sizes
    gx, yz = lax.axis_index("gx"), lax.axis_index("yz")
    wide_y = rows_y + EDGE
    stride = wide_y
    per_half = depth // EDGE

    inputs = (
        (coef_hbm, coef), (off_hbm, off_rows), (syn_hbm, syn_ref), (occ_hbm, occ),
        (core_hbm, core), (vext_hbm, vext),
    )
    loads = [pltpu.make_async_copy(src, dst, in_sems.at[n]) for n, (src, dst) in enumerate(inputs)]
    for load in loads:
        load.start()
    load_coef, load_off_rows, load_syn, load_occ, load_core, load_vext = loads

    after_x, before_x = gx < n_gx - 1, gx > 0
    after_y, before_y = yz < n_yz - 1, yz > 0
    next_x, next_y, last_x, last_y = (gx + 1, yz), (gx, yz + 1), (gx - 1, yz), (gx, yz - 1)
    odd = lax.rem(gx, 2) == 1
    even = jnp.logical_not(odd)
    alone, feeds, takes = odd & after_x, even & before_x, even & after_x
    barrier = pltpu.get_barrier_semaphore()
    neighbours = 0
    for there, device in ((after_x, next_x), (after_y, next_y), (before_x, last_x), (before_y, last_y)):
        @pl.when(there)
        def _(device=device):
            pl.semaphore_signal(barrier, inc=1, device_id=device, device_id_type=MESH)

        neighbours = neighbours + there.astype(jnp.int32)

    for ref in (from_y, halo_from_y):
        ref[:, REACH:, :] = jnp.zeros((ref.shape[0], EDGE - REACH, depth), F32)

    @pl.when(jnp.logical_not(before_x))
    def _():
        from_x[...] = jnp.zeros_like(from_x)

    @pl.when(jnp.logical_not(before_y))
    def _():
        from_y[...] = jnp.zeros_like(from_y)
        halo_from_y[...] = jnp.zeros_like(halo_from_y)

    @pl.when(jnp.logical_not(after_y))
    def _():
        for ref in (from_after, halo_from_after, vext_far, vext_corner):
            ref[...] = jnp.zeros_like(ref)

    def clear(slot, carry):
        for plane in range(EDGE + 3):
            padded[slot, pl.ds(stride * plane, rows_y), :] = jnp.zeros((rows_y, depth), F32)
        for plane in (0, EDGE + 1):
            padded[slot, pl.ds(stride * plane + rows_y, EDGE), :] = jnp.zeros((EDGE, depth), F32)
        return carry

    lax.fori_loop(0, slots, clear, 0)

    at_x, at_y, at_z, turn_to, turn_from = (rows_x + EDGE + n for n in range(5))
    load_off_rows.wait()
    begin_x = jnp.clip(off_rows[0:1, :] - gx * rows_x, 0, rows_x - 1)
    begin_y = jnp.clip(off_rows[1:2, :] - yz * rows_y, 0, rows_y - 1)
    plane = jnp.clip(iota((rows_x + EDGE, slots), 0) - begin_x + 1, 0, EDGE + 1)
    begin_z = off_rows[2:3, :]
    turn = begin_z - (iota((1, slots), 1) % per_half) * EDGE
    start_rows[: rows_x + EDGE, :slots] = plane * stride + rows_y - begin_y
    for n, value in enumerate((begin_x, begin_y, begin_z, turn & (depth - 1), (-turn) & (depth - 1))):
        start_rows[rows_x + EDGE + n : rows_x + EDGE + n + 1, :slots] = value
    table = pltpu.make_async_copy(start_rows, starts, table_sem)
    table.start()

    load_syn.wait()
    syn = syn_ref[...]
    lane = iota((EDGE, CUBE), 1)
    row = iota((EDGE, CUBE), 0)
    inside, outside = (lane % EDGE == row).astype(F32), (lane // EDGE == row).astype(F32)

    def exact(contract, right):
        return lax.dot_general(
            syn, right, (((contract,), (0,)), ((), ())), precision=HIGHEST, preferred_element_type=F32)

    by_i, by_j, by_a, by_b = exact(1, inside), exact(1, outside), exact(0, outside), exact(0, inside)
    for n in range(EDGE):
        rows = slice(n * EDGE, (n + 1) * EDGE)
        here = lane // EDGE == n
        for refs, value in (
            (kron, by_i[n : n + 1, :] * by_j),
            (back, by_b[n : n + 1, :] * by_a),
            (filt, jnp.where(here, by_b, 0.0)),
            (taps, jnp.where(here, by_i, 0.0)),
        ):
            high, low = split(value)
            refs[0, rows, :] = high
            refs[1, rows, :] = low

    load_occ.wait()
    load_coef.wait()
    swapped = swap_blocks(coef[...].reshape(slots * EDGE, CUBE).astype(F32)).astype(BF16)
    inner_high, inner_low = split(dot(kron[0], swapped) + dot(kron[1], swapped))
    psi[...] = dot(inner_high, filt[0]) + (dot(inner_low, filt[0]) + dot(inner_high, filt[1]))

    owner = iota((1, CUBE), 1) // EDGE
    weights = jnp.zeros((1, CUBE), F32)
    for f in range(slots):
        weights = jnp.where(owner == f, jnp.where(f < live[0], occ[f], 0.0), weights)
    square[...] = psi[...] * psi[...] * weights

    def place(n, carry):
        for half in range(CUBE // depth):
            f = half * per_half + n
            value = pltpu.roll(square[:, half * depth : (half + 1) * depth], starts[turn_to, f], 1)
            along = iota((1, depth), 1) - starts[at_z, f]
            value = jnp.where((along >= 0) & (along < EDGE), value, 0.0)
            for a in range(EDGE):
                padded[f, pl.ds(stride * (a + 1) + rows_y, EDGE), :] = value[a * EDGE : (a + 1) * EDGE, :]
        return carry

    issued = []

    def copy(there, src, dst, device, arrives):
        index = len(issued)
        descriptor = pltpu.make_async_remote_copy(
            src_ref=src, dst_ref=dst, send_sem=send_sems.at[index], recv_sem=recv_sems.at[index],
            device_id=device, device_id_type=MESH,
        )

        @pl.when(there)
        def _():
            descriptor.start()

        issued.append((there, descriptor))

        def landed():
            @pl.when(arrives)
            def _():
                descriptor.wait_recv()

        return landed

    groups = REACH // GROUP
    rest = rows_x - REACH
    edge, inner, far = pl.ds(0, EDGE), pl.ds(EDGE, rows_y - EDGE), pl.ds(rows_y, EDGE)
    edge_sent, far_sent = pl.ds(0, REACH), pl.ds(rows_y, REACH)
    spans = [pl.ds(g * GROUP, GROUP) for g in range(groups)]
    beyond = [pl.ds(rows_x + g * GROUP, GROUP) for g in range(groups)]
    others = pl.ds(REACH, rest)

    pl.semaphore_wait(barrier, neighbours)
    load_vext.wait()
    first = pl.ds(0, REACH)
    vext_in = copy(before_y, vext.at[first, edge_sent], vext_far.at[:, edge_sent], last_y, after_y)

    table.wait()
    lax.fori_loop(0, per_half, place, 0, unroll=2)

    def sum_planes(first, count, unit, own):
        def body(step, carry):
            x = first + step * unit
            totals = [None] * unit
            for f in range(slots):
                for n in range(unit):
                    rows = padded[f, pl.ds(starts[x + n, f], wide_y), :]
                    totals[n] = rows if f == 0 else totals[n] + rows
            for n in range(unit):
                if own:
                    partial[x + n, :rows_y, :] = totals[n][:rows_y] + core[x + n]
                    partial[x + n, rows_y:, :] = totals[n][rows_y:]
                else:
                    partial[x + n] = totals[n]
            return carry

        lax.fori_loop(0, count // unit, body, 0)

    load_core.wait()
    sum_planes(REACH, rest, 3, True)
    rest_in = copy(after_y, partial.at[others, far_sent], from_y.at[others, edge_sent], next_y, before_y)
    far_in, edge_in, inner_in, next_in = [], [], [], []
    for g in range(groups):
        sum_planes(rows_x + g * GROUP, GROUP, GROUP, False)
        far_in.append(copy(after_x, partial.at[beyond[g], far_sent], from_x.at[spans[g], far_sent], next_x, before_x))
        edge_in.append(copy(after_x, partial.at[beyond[g], edge], from_x.at[spans[g], edge], next_x, before_x))
        sum_planes(g * GROUP, GROUP, GROUP, True)
        for rows in (far_sent, edge):
            next_in.append(copy(feeds, partial.at[spans[g], rows], from_next.at[spans[g], rows], last_x, alone))
    vext_next_in = copy(feeds, vext.at[first, edge], vext_next, last_x, alone)

    onward_in, back_in, halo_onward_in, halo_back_in = [], [], [], []
    for g in range(groups):
        far_in[g]()
        side_far[spans[g]] = partial[spans[g], far, :] + from_x[spans[g], far, :]
        onward_in.append(copy(after_y, side_far.at[spans[g], edge_sent], from_y.at[spans[g], edge_sent], next_y, before_y))
        edge_in[g]()
        side_edge[spans[g]] = partial[spans[g], edge, :] + from_x[spans[g], edge, :]
        back_in.append(copy(before_y, side_edge.at[spans[g], edge_sent], from_after.at[spans[g], edge_sent], last_y, after_y))
    for g in range(groups):
        inner_in.append(copy(after_x, partial.at[beyond[g], inner], from_x.at[spans[g], inner], next_x, before_x))
    vext_in()
    vext_corner_in = copy(feeds & after_y, vext_far.at[:, edge_sent], vext_corner.at[:, edge_sent], last_x, alone & after_y)
    def potential(planes, rows, external, *densities):
        density = functools.reduce(jnp.add, densities)
        ext[planes, rows, :] = external + XC_COEF * jnp.exp2(jnp.log2(density) * (1.0 / 3.0))

    waits = []
    rest_in()
    potential(others, edge, vext[others, edge, :], partial[others, edge, :], from_y[others])
    waits.append(copy(before_y, ext.at[others, edge_sent], ext.at[others, far_sent], last_y, after_y))
    for g in range(groups):
        inner_in[g]()
        potential(spans[g], inner, vext[spans[g], inner, :], partial[spans[g], inner, :], from_x[spans[g], inner, :])
        waits.append(copy(before_x, ext.at[spans[g], inner], ext.at[beyond[g], inner], last_x, after_x))
    potential(others, inner, vext[others, inner, :], partial[others, inner, :])
    for g in range(groups):
        next_in[2 * g]()
        next_in[2 * g + 1]()

        @pl.when(alone)
        def _(g=g):
            halo_far[spans[g]] = partial[beyond[g], far, :] + from_next[spans[g], far, :]
            halo_edge[spans[g]] = partial[beyond[g], edge, :] + from_next[spans[g], edge, :]

        halo_onward_in.append(copy(
            alone & after_y, halo_far.at[spans[g], edge_sent], halo_from_y.at[spans[g], edge_sent], next_y, alone & before_y))
        halo_back_in.append(copy(
            alone & before_y, halo_edge.at[spans[g], edge_sent], halo_from_after.at[spans[g], edge_sent], last_y, alone & after_y))
        onward_in[g]()
        potential(spans[g], edge, vext[spans[g], edge, :], side_edge[spans[g]], from_y[spans[g]])
        waits.append(copy(odd, ext.at[spans[g], edge], ext.at[beyond[g], edge], last_x, takes))
        back_in[g]()
        potential(spans[g], far, vext_far[spans[g]], side_far[spans[g]], from_after[spans[g]])
        waits.append(copy(odd, ext.at[spans[g], far_sent], ext.at[beyond[g], far_sent], last_x, takes))
    vext_next_in()
    vext_corner_in()
    for g in range(groups):
        halo_onward_in[g]()
        halo_back_in[g]()

        @pl.when(alone)
        def _(g=g):
            potential(beyond[g], edge, vext_next[spans[g]], halo_edge[spans[g]], halo_from_y[spans[g]])
            potential(beyond[g], far, vext_corner[spans[g]], halo_far[spans[g]], halo_from_after[spans[g]])

    for landed in waits:
        landed()

    def collect(part, carry):
        rows = pl.ds(pl.multiple_of(part * CHUNK * EDGE, CHUNK * EDGE), CHUNK * EDGE)
        block = iota((1, depth), 1) // EDGE
        totals = []
        for half in range(CUBE // depth):
            total = None
            for n in range(per_half):
                f = half * per_half + n
                box = ext[pl.ds(starts[at_x, f] + part * CHUNK, CHUNK), pl.ds(starts[at_y, f], EDGE), :]
                box = pltpu.roll(box.reshape(CHUNK * EDGE, depth), starts[turn_from, f], 1)
                total = box if n == 0 else jnp.where(block == n, box, total)
            totals.append(total)
        high, low = split(jnp.concatenate(totals, axis=1) * psi[rows, :])
        value = dot(high, taps[0]) + (dot(high, taps[1]) + dot(low, taps[0]))
        high, low = split(jnp.where(iota((1, CUBE), 1) < live[0] * EDGE, value, 0.0))
        boxes[0, rows, :] = high
        boxes[1, rows, :] = low
        return carry

    lax.fori_loop(0, EDGE // CHUNK, collect, 0, unroll=4)
    for there, descriptor in issued:
        @pl.when(there)
        def _(descriptor=descriptor):
            descriptor.wait_send()


def deliver(boxes, back, ext, hpsi_hbm, pot_hbm, hpsi, sems):
    slots, _, _ = hpsi_hbm.shape
    rows_x, rows_y, _ = pot_hbm.shape
    pot_out = pltpu.make_async_copy(ext.at[pl.ds(0, rows_x), pl.ds(0, rows_y)], pot_hbm, sems.at[0])
    pot_out.start()
    high, low = boxes[0], boxes[1]
    result = dot(back[0], high) + (dot(back[0], low) + dot(back[1], high))
    hpsi[...] = swap_blocks(result).astype(BF16).reshape(slots, EDGE, CUBE)
    hpsi_out = pltpu.make_async_copy(hpsi, hpsi_hbm, sems.at[1])
    hpsi_out.start()
    pot_out.wait()
    hpsi_out.wait()


def shards(n_gx, n_yz, coeffs, occupation, box_offset, live_count, synthesis, v_ext, core_density):
    slots = coeffs.shape[0]
    rows_x, rows_y, depth = v_ext.shape
    wide_x, wide_y = rows_x + EDGE, rows_y + EDGE
    exchanges = 5 + 12 * (REACH // GROUP)
    vmem = pl.BlockSpec(memory_space=pltpu.VMEM)
    hbm = pl.BlockSpec(memory_space=pltpu.HBM)
    inputs = (occupation, box_offset.T, live_count, synthesis, coeffs, v_ext, core_density)
    boxes, back, ext = pl.pallas_call(
        functools.partial(kernel, (slots, rows_x, rows_y, depth, n_gx, n_yz)),
        out_shape=(
            pltpu.VMEM((2, CUBE, CUBE), BF16),
            pltpu.VMEM((2, CUBE, CUBE), BF16),
            pltpu.VMEM((wide_x, wide_y, depth), F32),
        ),
        in_specs=[hbm, hbm, pl.BlockSpec(memory_space=pltpu.SMEM), hbm, hbm, hbm, hbm],
        out_specs=(vmem, vmem, vmem),
        scratch_shapes=[
            pltpu.SMEM(occupation.shape, F32),
            pltpu.VMEM((3, slots), jnp.int32),
            pltpu.VMEM(synthesis.shape, F32),
            pltpu.VMEM(coeffs.shape, BF16),
            pltpu.VMEM(v_ext.shape, F32),
            pltpu.VMEM(v_ext.shape, F32),
            pltpu.VMEM((wide_x + 8, 128), jnp.int32),
            pltpu.SMEM((wide_x + 8, 128), jnp.int32),
            *[pltpu.VMEM((2, CUBE, CUBE), BF16)] * 3,
            *[pltpu.VMEM((CUBE, CUBE), F32)] * 2,
            pltpu.VMEM((slots, wide_y * (EDGE + 2) + rows_y, depth), F32),
            pltpu.VMEM((wide_x, wide_y, depth), F32),
            pltpu.VMEM((REACH, wide_y, depth), F32),
            pltpu.VMEM((rows_x, EDGE, depth), F32),
            pltpu.VMEM((REACH, EDGE, depth), F32),
            pltpu.VMEM((REACH, EDGE, depth), F32),
            pltpu.VMEM((REACH, wide_y, depth), F32),
            *[pltpu.VMEM((REACH, EDGE, depth), F32)] * 8,
            pltpu.SemaphoreType.DMA((len(inputs) - 1,)),
            pltpu.SemaphoreType.DMA,
            pltpu.SemaphoreType.DMA((exchanges,)),
            pltpu.SemaphoreType.DMA((exchanges,)),
        ],
        compiler_params=pltpu.CompilerParams(
            collective_id=0, has_side_effects=True, vmem_limit_bytes=40 * 1024 * 1024
        ),
    )(*(v if v is live_count else pltpu.with_memory_space_constraint(v, pltpu.HBM) for v in inputs))
    return pl.pallas_call(
        deliver,
        out_shape=(jax.ShapeDtypeStruct(coeffs.shape, BF16), jax.ShapeDtypeStruct(v_ext.shape, F32)),
        in_specs=[vmem, vmem, vmem],
        out_specs=(hbm, hbm),
        scratch_shapes=[pltpu.VMEM(coeffs.shape, BF16), pltpu.SemaphoreType.DMA((2,))],
        compiler_params=pltpu.CompilerParams(vmem_limit_bytes=16 * 1024 * 1024),
    )(boxes, back, ext)


def solution(mesh):
    placed = (
        P(("gx", "yz"), None, None),
        P(("gx", "yz")),
        P(("gx", "yz"), None),
        P(("gx", "yz")),
        P(),
        P("gx", "yz", None),
        P("gx", "yz", None),
    )
    return jax.shard_map(
        functools.partial(shards, mesh.shape["gx"], mesh.shape["yz"]),
        mesh=mesh,
        in_specs=placed,
        out_specs=(P(("gx", "yz"), None, None), P("gx", "yz", None)),
        check_vma=False,
    )
```

```python
import functools

import jax
import jax.numpy as jnp
from jax import lax
from jax.experimental import pallas as pl
from jax.experimental.pallas import tpu as pltpu
from jax.sharding import PartitionSpec as P

XC_COEF = -0.9847450218426964
EDGE = 16
CUBE = EDGE * EDGE
REACH = EDGE - 1
CHUNK = 4
GROUP = 5
F32 = jnp.float32
BF16 = jnp.bfloat16
HIGHEST = lax.Precision.HIGHEST
MESH = pl.DeviceIdType.MESH


def iota(shape, dim):
    return lax.broadcasted_iota(jnp.int32, shape, dim)


def split(value):
    high = value.astype(BF16)
    low = (value - high.astype(F32)).astype(BF16)
    return high, low


def dot(left, right):
    return lax.dot_general(left, right, (((1,), (0,)), ((), ())), preferred_element_type=F32)


def swap_blocks(value):
    half = EDGE // 2
    tiles = [
        [[value[p * EDGE : (p + 1) * EDGE, t * 128 : (t + 1) * 128] for p in range(u * half, (u + 1) * half)] for t in range(2)]
        for u in range(2)
    ]
    block = iota((EDGE, 128), 1) // EDGE
    rows = []
    for u in range(2):
        parts = []
        for t in range(2):
            part = tiles[t][u]
            for step in (1, 2, 4):
                there = (block & step) != 0
                part = [
                    jnp.where(there, part[p], pltpu.roll(part[p - step], 128 - step * EDGE, 1))
                    if p & step
                    else jnp.where(there, pltpu.roll(part[p + step], step * EDGE, 1), part[p])
                    for p in range(half)
                ]
            parts.append(jnp.concatenate(part, axis=0))
        rows.append(jnp.concatenate(parts, axis=1))
    return jnp.concatenate(rows, axis=0)


def kernel(
    sizes,
    occ_hbm, off_hbm, live, syn_hbm, coef_hbm, vext_hbm, core_hbm,
    boxes, back, ext,
    occ, off_rows, syn_ref, coef, vext, core, start_rows, starts,
    kron, filt, taps, psi, square, padded, partial, from_x, from_y, from_after, vext_far,
    from_next, vext_next, vext_corner, side_far, side_edge, halo_far, halo_edge, halo_from_y, halo_from_after,
    in_sems, table_sem, send_sems, recv_sems,
):
    slots, rows_x, rows_y, depth, n_gx, n_yz = sizes
    gx, yz = lax.axis_index("gx"), lax.axis_index("yz")
    wide_y = rows_y + EDGE
    stride = wide_y
    per_half = depth // EDGE

    inputs = (
        (coef_hbm, coef), (off_hbm, off_rows), (syn_hbm, syn_ref), (occ_hbm, occ),
        (core_hbm, core), (vext_hbm, vext),
    )
    loads = [pltpu.make_async_copy(src, dst, in_sems.at[n]) for n, (src, dst) in enumerate(inputs)]
    for load in loads:
        load.start()
    load_coef, load_off_rows, load_syn, load_occ, load_core, load_vext = loads

    after_x, before_x = gx < n_gx - 1, gx > 0
    after_y, before_y = yz < n_yz - 1, yz > 0
    next_x, next_y, last_x, last_y = (gx + 1, yz), (gx, yz + 1), (gx - 1, yz), (gx, yz - 1)
    odd = lax.rem(gx, 2) == 1
    even = jnp.logical_not(odd)
    alone, feeds, takes = odd & after_x, even & before_x, even & after_x
    barrier = pltpu.get_barrier_semaphore()
    neighbours = 0
    for there, device in ((after_x, next_x), (after_y, next_y), (before_x, last_x), (before_y, last_y)):
        @pl.when(there)
        def _(device=device):
            pl.semaphore_signal(barrier, inc=1, device_id=device, device_id_type=MESH)

        neighbours = neighbours + there.astype(jnp.int32)

    for ref in (from_y, halo_from_y):
        ref[:, REACH:, :] = jnp.zeros((ref.shape[0], EDGE - REACH, depth), F32)

    @pl.when(jnp.logical_not(before_x))
    def _():
        from_x[...] = jnp.zeros_like(from_x)

    @pl.when(jnp.logical_not(before_y))
    def _():
        from_y[...] = jnp.zeros_like(from_y)
        halo_from_y[...] = jnp.zeros_like(halo_from_y)

    @pl.when(jnp.logical_not(after_y))
    def _():
        for ref in (from_after, halo_from_after, vext_far, vext_corner):
            ref[...] = jnp.zeros_like(ref)

    def clear(slot, carry):
        for plane in range(EDGE + 3):
            padded[slot, pl.ds(stride * plane, rows_y), :] = jnp.zeros((rows_y, depth), F32)
        for plane in (0, EDGE + 1):
            padded[slot, pl.ds(stride * plane + rows_y, EDGE), :] = jnp.zeros((EDGE, depth), F32)
        return carry

    lax.fori_loop(0, slots, clear, 0)

    at_x, at_y, at_z, turn_to, turn_from = (rows_x + EDGE + n for n in range(5))
    load_off_rows.wait()
    begin_x = jnp.clip(off_rows[0:1, :] - gx * rows_x, 0, rows_x - 1)
    begin_y = jnp.clip(off_rows[1:2, :] - yz * rows_y, 0, rows_y - 1)
    plane = jnp.clip(iota((rows_x + EDGE, slots), 0) - begin_x + 1, 0, EDGE + 1)
    begin_z = off_rows[2:3, :]
    turn = begin_z - (iota((1, slots), 1) % per_half) * EDGE
    start_rows[: rows_x + EDGE, :slots] = plane * stride + rows_y - begin_y
    for n, value in enumerate((begin_x, begin_y, begin_z, turn & (depth - 1), (-turn) & (depth - 1))):
        start_rows[rows_x + EDGE + n : rows_x + EDGE + n + 1, :slots] = value
    table = pltpu.make_async_copy(start_rows, starts, table_sem)
    table.start()

    load_syn.wait()
    syn = syn_ref[...]
    lane = iota((EDGE, CUBE), 1)
    row = iota((EDGE, CUBE), 0)
    inside, outside = (lane % EDGE == row).astype(F32), (lane // EDGE == row).astype(F32)

    def exact(contract, right):
        return lax.dot_general(
            syn, right, (((contract,), (0,)), ((), ())), precision=HIGHEST, preferred_element_type=F32)

    by_i, by_j, by_a, by_b = exact(1, inside), exact(1, outside), exact(0, outside), exact(0, inside)
    for n in range(EDGE):
        rows = slice(n * EDGE, (n + 1) * EDGE)
        here = lane // EDGE == n
        for refs, value in (
            (kron, by_i[n : n + 1, :] * by_j),
            (back, by_b[n : n + 1, :] * by_a),
            (filt, jnp.where(here, by_b, 0.0)),
            (taps, jnp.where(here, by_i, 0.0)),
        ):
            high, low = split(value)
            refs[0, rows, :] = high
            refs[1, rows, :] = low

    load_occ.wait()
    load_coef.wait()
    swapped = swap_blocks(coef[...].reshape(slots * EDGE, CUBE).astype(F32)).astype(BF16)
    inner_high, inner_low = split(dot(kron[0], swapped) + dot(kron[1], swapped))
    psi[...] = dot(inner_high, filt[0]) + (dot(inner_low, filt[0]) + dot(inner_high, filt[1]))

    owner = iota((1, CUBE), 1) // EDGE
    weights = jnp.zeros((1, CUBE), F32)
    for f in range(slots):
        weights = jnp.where(owner == f, jnp.where(f < live[0], occ[f], 0.0), weights)
    square[...] = psi[...] * psi[...] * weights

    def place(n, carry):
        for half in range(CUBE // depth):
            f = half * per_half + n
            value = pltpu.roll(square[:, half * depth : (half + 1) * depth], starts[turn_to, f], 1)
            along = iota((1, depth), 1) - starts[at_z, f]
            value = jnp.where((along >= 0) & (along < EDGE), value, 0.0)
            for a in range(EDGE):
                padded[f, pl.ds(stride * (a + 1) + rows_y, EDGE), :] = value[a * EDGE : (a + 1) * EDGE, :]
        return carry

    issued = []

    def copy(there, src, dst, device, arrives):
        index = len(issued)
        descriptor = pltpu.make_async_remote_copy(
            src_ref=src, dst_ref=dst, send_sem=send_sems.at[index], recv_sem=recv_sems.at[index],
            device_id=device, device_id_type=MESH,
        )

        @pl.when(there)
        def _():
            descriptor.start()

        issued.append((there, descriptor))

        def landed():
            @pl.when(arrives)
            def _():
                descriptor.wait_recv()

        return landed

    groups = REACH // GROUP
    rest = rows_x - REACH
    edge, inner, far = pl.ds(0, EDGE), pl.ds(EDGE, rows_y - EDGE), pl.ds(rows_y, EDGE)
    edge_sent, far_sent = pl.ds(0, REACH), pl.ds(rows_y, REACH)
    spans = [pl.ds(g * GROUP, GROUP) for g in range(groups)]
    beyond = [pl.ds(rows_x + g * GROUP, GROUP) for g in range(groups)]
    others = pl.ds(REACH, rest)

    pl.semaphore_wait(barrier, neighbours)
    load_vext.wait()
    first = pl.ds(0, REACH)
    vext_in = copy(before_y, vext.at[first, edge_sent], vext_far.at[:, edge_sent], last_y, after_y)

    table.wait()
    lax.fori_loop(0, per_half, place, 0, unroll=4)

    def sum_planes(first, count, unit, own):
        def body(step, carry):
            x = first + step * unit
            totals = [None] * unit
            for f in range(slots):
                for n in range(unit):
                    rows = padded[f, pl.ds(starts[x + n, f], wide_y), :]
                    totals[n] = rows if f == 0 else totals[n] + rows
            for n in range(unit):
                if own:
                    partial[x + n, :rows_y, :] = totals[n][:rows_y] + core[x + n]
                    partial[x + n, rows_y:, :] = totals[n][rows_y:]
                else:
                    partial[x + n] = totals[n]
            return carry

        lax.fori_loop(0, count // unit, body, 0)

    load_core.wait()
    sum_planes(REACH, rest, 3, True)
    rest_in = copy(after_y, partial.at[others, far_sent], from_y.at[others, edge_sent], next_y, before_y)
    far_in, edge_in, inner_in, next_in = [], [], [], []
    for g in range(groups):
        sum_planes(g * GROUP, GROUP, GROUP, True)
        for rows in (far_sent, edge):
            next_in.append(copy(feeds, partial.at[spans[g], rows], from_next.at[spans[g], rows], last_x, alone))
        sum_planes(rows_x + g * GROUP, GROUP, GROUP, False)
        far_in.append(copy(
            after_x, partial.at[beyond[g], far_sent], from_x.at[spans[g], far_sent], next_x, before_x))
        edge_in.append(copy(after_x, partial.at[beyond[g], edge], from_x.at[spans[g], edge], next_x, before_x))

    vext_next_in = copy(feeds, vext.at[first, edge], vext_next, last_x, alone)

    onward_in, back_in, halo_onward_in, halo_back_in = [], [], [], []
    for g in range(groups):
        far_in[g]()
        side_far[spans[g]] = partial[spans[g], far, :] + from_x[spans[g], far, :]
        onward_in.append(copy(after_y, side_far.at[spans[g], edge_sent], from_y.at[spans[g], edge_sent], next_y, before_y))
        edge_in[g]()
        side_edge[spans[g]] = partial[spans[g], edge, :] + from_x[spans[g], edge, :]
        back_in.append(copy(before_y, side_edge.at[spans[g], edge_sent], from_after.at[spans[g], edge_sent], last_y, after_y))
    for g in range(groups):
        inner_in.append(copy(after_x, partial.at[beyond[g], inner], from_x.at[spans[g], inner], next_x, before_x))
    vext_in()
    vext_corner_in = copy(feeds & after_y, vext_far.at[:, edge_sent], vext_corner.at[:, edge_sent], last_x, alone & after_y)
    def potential(planes, rows, external, *densities):
        density = functools.reduce(jnp.add, densities)
        ext[planes, rows, :] = external + XC_COEF * jnp.exp2(jnp.log2(density) * (1.0 / 3.0))

    waits = []
    rest_in()
    potential(others, edge, vext[others, edge, :], partial[others, edge, :], from_y[others])
    waits.append(copy(before_y, ext.at[others, edge_sent], ext.at[others, far_sent], last_y, after_y))
    for g in range(groups):
        inner_in[g]()
        potential(spans[g], inner, vext[spans[g], inner, :], partial[spans[g], inner, :], from_x[spans[g], inner, :])
        waits.append(copy(before_x, ext.at[spans[g], inner], ext.at[beyond[g], inner], last_x, after_x))
    potential(others, inner, vext[others, inner, :], partial[others, inner, :])
    for g in range(groups):
        next_in[2 * g]()
        next_in[2 * g + 1]()

        @pl.when(alone)
        def _(g=g):
            halo_far[spans[g]] = partial[beyond[g], far, :] + from_next[spans[g], far, :]
            halo_edge[spans[g]] = partial[beyond[g], edge, :] + from_next[spans[g], edge, :]

        halo_onward_in.append(copy(
            alone & after_y, halo_far.at[spans[g], edge_sent], halo_from_y.at[spans[g], edge_sent], next_y, alone & before_y))
        halo_back_in.append(copy(
            alone & before_y, halo_edge.at[spans[g], edge_sent], halo_from_after.at[spans[g], edge_sent], last_y, alone & after_y))
        onward_in[g]()
        potential(spans[g], edge, vext[spans[g], edge, :], side_edge[spans[g]], from_y[spans[g]])
        waits.append(copy(odd, ext.at[spans[g], edge], ext.at[beyond[g], edge], last_x, takes))
        back_in[g]()
        potential(spans[g], far, vext_far[spans[g]], side_far[spans[g]], from_after[spans[g]])
        waits.append(copy(odd, ext.at[spans[g], far_sent], ext.at[beyond[g], far_sent], last_x, takes))
    vext_next_in()
    vext_corner_in()
    for g in range(groups):
        halo_onward_in[g]()
        halo_back_in[g]()

        @pl.when(alone)
        def _(g=g):
            potential(beyond[g], edge, vext_next[spans[g]], halo_edge[spans[g]], halo_from_y[spans[g]])
            potential(beyond[g], far, vext_corner[spans[g]], halo_far[spans[g]], halo_from_after[spans[g]])

    for landed in waits:
        landed()

    def collect(part, carry):
        rows = pl.ds(pl.multiple_of(part * CHUNK * EDGE, CHUNK * EDGE), CHUNK * EDGE)
        block = iota((1, depth), 1) // EDGE
        totals = []
        for half in range(CUBE // depth):
            total = None
            for n in range(per_half):
                f = half * per_half + n
                box = ext[pl.ds(starts[at_x, f] + part * CHUNK, CHUNK), pl.ds(starts[at_y, f], EDGE), :]
                box = pltpu.roll(box.reshape(CHUNK * EDGE, depth), starts[turn_from, f], 1)
                total = box if n == 0 else jnp.where(block == n, box, total)
            totals.append(total)
        high, low = split(jnp.concatenate(totals, axis=1) * psi[rows, :])
        value = dot(high, taps[0]) + (dot(high, taps[1]) + dot(low, taps[0]))
        high, low = split(jnp.where(iota((1, CUBE), 1) < live[0] * EDGE, value, 0.0))
        boxes[0, rows, :] = high
        boxes[1, rows, :] = low
        return carry

    lax.fori_loop(0, EDGE // CHUNK, collect, 0, unroll=4)
    for there, descriptor in issued:
        @pl.when(there)
        def _(descriptor=descriptor):
            descriptor.wait_send()


def deliver(boxes, back, ext, hpsi_hbm, pot_hbm, hpsi, sems):
    slots, _, _ = hpsi_hbm.shape
    rows_x, rows_y, _ = pot_hbm.shape
    pot_out = pltpu.make_async_copy(ext.at[pl.ds(0, rows_x), pl.ds(0, rows_y)], pot_hbm, sems.at[0])
    pot_out.start()
    high, low = boxes[0], boxes[1]
    result = dot(back[0], high) + (dot(back[0], low) + dot(back[1], high))
    hpsi[...] = swap_blocks(result).astype(BF16).reshape(slots, EDGE, CUBE)
    hpsi_out = pltpu.make_async_copy(hpsi, hpsi_hbm, sems.at[1])
    hpsi_out.start()
    pot_out.wait()
    hpsi_out.wait()


def shards(n_gx, n_yz, coeffs, occupation, box_offset, live_count, synthesis, v_ext, core_density):
    slots = coeffs.shape[0]
    rows_x, rows_y, depth = v_ext.shape
    wide_x, wide_y = rows_x + EDGE, rows_y + EDGE
    exchanges = 5 + 12 * (REACH // GROUP)
    vmem = pl.BlockSpec(memory_space=pltpu.VMEM)
    hbm = pl.BlockSpec(memory_space=pltpu.HBM)
    inputs = (occupation, box_offset.T, live_count, synthesis, coeffs, v_ext, core_density)
    boxes, back, ext = pl.pallas_call(
        functools.partial(kernel, (slots, rows_x, rows_y, depth, n_gx, n_yz)),
        out_shape=(
            pltpu.VMEM((2, CUBE, CUBE), BF16),
            pltpu.VMEM((2, CUBE, CUBE), BF16),
            pltpu.VMEM((wide_x, wide_y, depth), F32),
        ),
        in_specs=[hbm, hbm, pl.BlockSpec(memory_space=pltpu.SMEM), hbm, hbm, hbm, hbm],
        out_specs=(vmem, vmem, vmem),
        scratch_shapes=[
            pltpu.SMEM(occupation.shape, F32),
            pltpu.VMEM((3, slots), jnp.int32),
            pltpu.VMEM(synthesis.shape, F32),
            pltpu.VMEM(coeffs.shape, BF16),
            pltpu.VMEM(v_ext.shape, F32),
            pltpu.VMEM(v_ext.shape, F32),
            pltpu.VMEM((wide_x + 8, 128), jnp.int32),
            pltpu.SMEM((wide_x + 8, 128), jnp.int32),
            *[pltpu.VMEM((2, CUBE, CUBE), BF16)] * 3,
            *[pltpu.VMEM((CUBE, CUBE), F32)] * 2,
            pltpu.VMEM((slots, wide_y * (EDGE + 2) + rows_y, depth), F32),
            pltpu.VMEM((wide_x, wide_y, depth), F32),
            pltpu.VMEM((REACH, wide_y, depth), F32),
            pltpu.VMEM((rows_x, EDGE, depth), F32),
            pltpu.VMEM((REACH, EDGE, depth), F32),
            pltpu.VMEM((REACH, EDGE, depth), F32),
            pltpu.VMEM((REACH, wide_y, depth), F32),
            *[pltpu.VMEM((REACH, EDGE, depth), F32)] * 8,
            pltpu.SemaphoreType.DMA((len(inputs) - 1,)),
            pltpu.SemaphoreType.DMA,
            pltpu.SemaphoreType.DMA((exchanges,)),
            pltpu.SemaphoreType.DMA((exchanges,)),
        ],
        compiler_params=pltpu.CompilerParams(
            collective_id=0, has_side_effects=True, vmem_limit_bytes=40 * 1024 * 1024
        ),
    )(*(v if v is live_count else pltpu.with_memory_space_constraint(v, pltpu.HBM) for v in inputs))
    return pl.pallas_call(
        deliver,
        out_shape=(jax.ShapeDtypeStruct(coeffs.shape, BF16), jax.ShapeDtypeStruct(v_ext.shape, F32)),
        in_specs=[vmem, vmem, vmem],
        out_specs=(hbm, hbm),
        scratch_shapes=[pltpu.VMEM(coeffs.shape, BF16), pltpu.SemaphoreType.DMA((2,))],
        compiler_params=pltpu.CompilerParams(vmem_limit_bytes=16 * 1024 * 1024),
    )(boxes, back, ext)


def solution(mesh):
    placed = (
        P(("gx", "yz"), None, None),
        P(("gx", "yz")),
        P(("gx", "yz"), None),
        P(("gx", "yz")),
        P(),
        P("gx", "yz", None),
        P("gx", "yz", None),
    )
    return jax.shard_map(
        functools.partial(shards, mesh.shape["gx"], mesh.shape["yz"]),
        mesh=mesh,
        in_specs=placed,
        out_specs=(P(("gx", "yz"), None, None), P("gx", "yz", None)),
        check_vma=False,
    )
```

```python
import functools

import jax
import jax.numpy as jnp
from jax import lax
from jax.experimental import pallas as pl
from jax.experimental.pallas import tpu as pltpu
from jax.sharding import PartitionSpec as P

XC_COEF = -0.9847450218426964
EDGE = 16
CUBE = EDGE * EDGE
REACH = EDGE - 1
CHUNK = 4
GROUP = 5
F32 = jnp.float32
BF16 = jnp.bfloat16
HIGHEST = lax.Precision.HIGHEST
MESH = pl.DeviceIdType.MESH


def iota(shape, dim):
    return lax.broadcasted_iota(jnp.int32, shape, dim)


def split(value):
    high = value.astype(BF16)
    low = (value - high.astype(F32)).astype(BF16)
    return high, low


def dot(left, right):
    return lax.dot_general(left, right, (((1,), (0,)), ((), ())), preferred_element_type=F32)


def swap_half(value):
    half = EDGE // 2
    block = iota((EDGE, 128), 1) // EDGE
    parts = []
    for t in range(2):
        part = [value[p * EDGE : (p + 1) * EDGE] for p in range(t * half, (t + 1) * half)]
        for step in (1, 2, 4):
            there = (block & step) != 0
            part = [
                jnp.where(there, part[p], pltpu.roll(part[p - step], 128 - step * EDGE, 1))
                if p & step
                else jnp.where(there, pltpu.roll(part[p + step], step * EDGE, 1), part[p])
                for p in range(half)
            ]
        parts.append(jnp.concatenate(part, axis=0))
    return jnp.concatenate(parts, axis=1)


def swap_blocks(value):
    return jnp.concatenate([swap_half(value[:, :128]), swap_half(value[:, 128:])], axis=0)


def kernel(
    sizes,
    occ_hbm, off_hbm, live, syn_hbm, coef_hbm, vext_hbm, core_hbm,
    boxes, back, ext,
    occ, off_rows, syn_ref, coef, vext, core, start_rows, starts,
    kron, filt, taps, psi, square, padded, partial, from_x, from_y, from_after, vext_far,
    from_next, vext_next, vext_corner, side_far, side_edge, halo_far, halo_edge, halo_from_y, halo_from_after,
    in_sems, table_sem, send_sems, recv_sems,
):
    slots, rows_x, rows_y, depth, n_gx, n_yz = sizes
    gx, yz = lax.axis_index("gx"), lax.axis_index("yz")
    wide_y = rows_y + EDGE
    stride = wide_y
    per_half = depth // EDGE

    inputs = (
        (coef_hbm, coef), (off_hbm, off_rows), (syn_hbm, syn_ref), (occ_hbm, occ),
        (core_hbm, core), (vext_hbm, vext),
    )
    loads = [pltpu.make_async_copy(src, dst, in_sems.at[n]) for n, (src, dst) in enumerate(inputs)]
    for load in loads:
        load.start()
    load_coef, load_off_rows, load_syn, load_occ, load_core, load_vext = loads

    after_x, before_x = gx < n_gx - 1, gx > 0
    after_y, before_y = yz < n_yz - 1, yz > 0
    next_x, next_y, last_x, last_y = (gx + 1, yz), (gx, yz + 1), (gx - 1, yz), (gx, yz - 1)
    odd = lax.rem(gx, 2) == 1
    even = jnp.logical_not(odd)
    alone, feeds, takes = odd & after_x, even & before_x, even & after_x
    barrier = pltpu.get_barrier_semaphore()
    neighbours = 0
    for there, device in ((after_x, next_x), (after_y, next_y), (before_x, last_x), (before_y, last_y)):
        @pl.when(there)
        def _(device=device):
            pl.semaphore_signal(barrier, inc=1, device_id=device, device_id_type=MESH)

        neighbours = neighbours + there.astype(jnp.int32)

    for ref in (from_y, halo_from_y):
        ref[:, REACH:, :] = jnp.zeros((ref.shape[0], EDGE - REACH, depth), F32)

    @pl.when(jnp.logical_not(before_x))
    def _():
        from_x[...] = jnp.zeros_like(from_x)

    @pl.when(jnp.logical_not(before_y))
    def _():
        from_y[...] = jnp.zeros_like(from_y)
        halo_from_y[...] = jnp.zeros_like(halo_from_y)

    @pl.when(jnp.logical_not(after_y))
    def _():
        for ref in (from_after, halo_from_after, vext_far, vext_corner):
            ref[...] = jnp.zeros_like(ref)

    def clear(slot, carry):
        for plane in range(EDGE + 3):
            padded[slot, pl.ds(stride * plane, rows_y), :] = jnp.zeros((rows_y, depth), F32)
        for plane in (0, EDGE + 1):
            padded[slot, pl.ds(stride * plane + rows_y, EDGE), :] = jnp.zeros((EDGE, depth), F32)
        return carry

    lax.fori_loop(0, slots, clear, 0)

    at_x, at_y, at_z, turn_to, turn_from = (rows_x + EDGE + n for n in range(5))
    load_off_rows.wait()
    begin_x = jnp.clip(off_rows[0:1, :] - gx * rows_x, 0, rows_x - 1)
    begin_y = jnp.clip(off_rows[1:2, :] - yz * rows_y, 0, rows_y - 1)
    plane = jnp.clip(iota((rows_x + EDGE, slots), 0) - begin_x + 1, 0, EDGE + 1)
    begin_z = off_rows[2:3, :]
    turn = begin_z - (iota((1, slots), 1) % per_half) * EDGE
    start_rows[: rows_x + EDGE, :slots] = plane * stride + rows_y - begin_y
    for n, value in enumerate((begin_x, begin_y, begin_z, turn & (depth - 1), (-turn) & (depth - 1))):
        start_rows[rows_x + EDGE + n : rows_x + EDGE + n + 1, :slots] = value
    table = pltpu.make_async_copy(start_rows, starts, table_sem)
    table.start()

    load_syn.wait()
    syn = syn_ref[...]
    lane = iota((EDGE, CUBE), 1)
    row = iota((EDGE, CUBE), 0)
    inside, outside = (lane % EDGE == row).astype(F32), (lane // EDGE == row).astype(F32)

    def exact(contract, right):
        return lax.dot_general(
            syn, right, (((contract,), (0,)), ((), ())), precision=HIGHEST, preferred_element_type=F32)

    by_i, by_j, by_a, by_b = exact(1, inside), exact(1, outside), exact(0, outside), exact(0, inside)
    for n in range(EDGE):
        rows = slice(n * EDGE, (n + 1) * EDGE)
        here = lane // EDGE == n
        for refs, value in (
            (kron, by_i[n : n + 1, :] * by_j),
            (back, by_b[n : n + 1, :] * by_a),
            (filt, jnp.where(here, by_b, 0.0)),
            (taps, jnp.where(here, by_i, 0.0)),
        ):
            high, low = split(value)
            refs[0, rows, :] = high
            refs[1, rows, :] = low

    load_occ.wait()
    load_coef.wait()
    swapped = swap_blocks(coef[...].reshape(slots * EDGE, CUBE).astype(F32)).astype(BF16)
    inner_high, inner_low = split(dot(kron[0], swapped) + dot(kron[1], swapped))
    psi[...] = dot(inner_high, filt[0]) + (dot(inner_low, filt[0]) + dot(inner_high, filt[1]))

    owner = iota((1, CUBE), 1) // EDGE
    weights = jnp.zeros((1, CUBE), F32)
    for f in range(slots):
        weights = jnp.where(owner == f, jnp.where(f < live[0], occ[f], 0.0), weights)
    square[...] = psi[...] * psi[...] * weights

    def place(n, carry):
        for half in range(CUBE // depth):
            f = half * per_half + n
            value = pltpu.roll(square[:, half * depth : (half + 1) * depth], starts[turn_to, f], 1)
            along = iota((1, depth), 1) - starts[at_z, f]
            value = jnp.where((along >= 0) & (along < EDGE), value, 0.0)
            for a in range(EDGE):
                padded[f, pl.ds(stride * (a + 1) + rows_y, EDGE), :] = value[a * EDGE : (a + 1) * EDGE, :]
        return carry

    issued = []

    def copy(there, src, dst, device, arrives):
        index = len(issued)
        descriptor = pltpu.make_async_remote_copy(
            src_ref=src, dst_ref=dst, send_sem=send_sems.at[index], recv_sem=recv_sems.at[index],
            device_id=device, device_id_type=MESH,
        )

        @pl.when(there)
        def _():
            descriptor.start()

        issued.append((there, descriptor))

        def landed():
            @pl.when(arrives)
            def _():
                descriptor.wait_recv()

        return landed

    groups = REACH // GROUP
    rest = rows_x - REACH
    edge, inner, far = pl.ds(0, EDGE), pl.ds(EDGE, rows_y - EDGE), pl.ds(rows_y, EDGE)
    edge_sent, far_sent = pl.ds(0, REACH), pl.ds(rows_y, REACH)
    spans = [pl.ds(g * GROUP, GROUP) for g in range(groups)]
    beyond = [pl.ds(rows_x + g * GROUP, GROUP) for g in range(groups)]
    others = pl.ds(REACH, rest)

    pl.semaphore_wait(barrier, neighbours)
    load_vext.wait()
    first = pl.ds(0, REACH)
    vext_in = copy(before_y, vext.at[first, edge_sent], vext_far.at[:, edge_sent], last_y, after_y)

    table.wait()
    lax.fori_loop(0, per_half, place, 0, unroll=4)

    def sum_planes(first, count, unit, own):
        def body(step, carry):
            x = first + step * unit
            totals = [None] * unit
            for f in range(slots):
                for n in range(unit):
                    rows = padded[f, pl.ds(starts[x + n, f], wide_y), :]
                    totals[n] = rows if f == 0 else totals[n] + rows
            for n in range(unit):
                if own:
                    partial[x + n, :rows_y, :] = totals[n][:rows_y] + core[x + n]
                    partial[x + n, rows_y:, :] = totals[n][rows_y:]
                else:
                    partial[x + n] = totals[n]
            return carry

        lax.fori_loop(0, count // unit, body, 0)

    load_core.wait()
    sum_planes(REACH, rest, 3, True)
    rest_in = copy(after_y, partial.at[others, far_sent], from_y.at[others, edge_sent], next_y, before_y)
    far_in, edge_in, inner_in, next_in = [], [], [], []
    for g in range(groups):
        sum_planes(g * GROUP, GROUP, GROUP, True)
        for rows in (far_sent, edge):
            next_in.append(copy(feeds, partial.at[spans[g], rows], from_next.at[spans[g], rows], last_x, alone))
        sum_planes(rows_x + g * GROUP, GROUP, GROUP, False)
        far_in.append(copy(
            after_x, partial.at[beyond[g], far_sent], from_x.at[spans[g], far_sent], next_x, before_x))
        edge_in.append(copy(after_x, partial.at[beyond[g], edge], from_x.at[spans[g], edge], next_x, before_x))

    vext_next_in = copy(feeds, vext.at[first, edge], vext_next, last_x, alone)

    onward_in, back_in, halo_onward_in, halo_back_in = [], [], [], []
    for g in range(groups):
        far_in[g]()
        side_far[spans[g]] = partial[spans[g], far, :] + from_x[spans[g], far, :]
        onward_in.append(copy(after_y, side_far.at[spans[g], edge_sent], from_y.at[spans[g], edge_sent], next_y, before_y))
        edge_in[g]()
        side_edge[spans[g]] = partial[spans[g], edge, :] + from_x[spans[g], edge, :]
        back_in.append(copy(before_y, side_edge.at[spans[g], edge_sent], from_after.at[spans[g], edge_sent], last_y, after_y))
    for g in range(groups):
        inner_in.append(copy(after_x, partial.at[beyond[g], inner], from_x.at[spans[g], inner], next_x, before_x))
    vext_in()
    vext_corner_in = copy(feeds & after_y, vext_far.at[:, edge_sent], vext_corner.at[:, edge_sent], last_x, alone & after_y)
    def potential(planes, rows, external, *densities):
        density = functools.reduce(jnp.add, densities)
        ext[planes, rows, :] = external + XC_COEF * jnp.exp2(jnp.log2(density) * (1.0 / 3.0))

    waits = []
    rest_in()
    potential(others, edge, vext[others, edge, :], partial[others, edge, :], from_y[others])
    waits.append(copy(before_y, ext.at[others, edge_sent], ext.at[others, far_sent], last_y, after_y))
    for g in range(groups):
        inner_in[g]()
        potential(spans[g], inner, vext[spans[g], inner, :], partial[spans[g], inner, :], from_x[spans[g], inner, :])
        waits.append(copy(before_x, ext.at[spans[g], inner], ext.at[beyond[g], inner], last_x, after_x))
    potential(others, inner, vext[others, inner, :], partial[others, inner, :])
    for g in range(groups):
        next_in[2 * g]()
        next_in[2 * g + 1]()

        @pl.when(alone)
        def _(g=g):
            halo_far[spans[g]] = partial[beyond[g], far, :] + from_next[spans[g], far, :]
            halo_edge[spans[g]] = partial[beyond[g], edge, :] + from_next[spans[g], edge, :]

        halo_onward_in.append(copy(
            alone & after_y, halo_far.at[spans[g], edge_sent], halo_from_y.at[spans[g], edge_sent], next_y, alone & before_y))
        halo_back_in.append(copy(
            alone & before_y, halo_edge.at[spans[g], edge_sent], halo_from_after.at[spans[g], edge_sent], last_y, alone & after_y))
        onward_in[g]()
        potential(spans[g], edge, vext[spans[g], edge, :], side_edge[spans[g]], from_y[spans[g]])
        waits.append(copy(odd, ext.at[spans[g], edge], ext.at[beyond[g], edge], last_x, takes))
        back_in[g]()
        potential(spans[g], far, vext_far[spans[g]], side_far[spans[g]], from_after[spans[g]])
        waits.append(copy(odd, ext.at[spans[g], far_sent], ext.at[beyond[g], far_sent], last_x, takes))
    vext_next_in()
    vext_corner_in()
    for g in range(groups):
        halo_onward_in[g]()
        halo_back_in[g]()

        @pl.when(alone)
        def _(g=g):
            potential(beyond[g], edge, vext_next[spans[g]], halo_edge[spans[g]], halo_from_y[spans[g]])
            potential(beyond[g], far, vext_corner[spans[g]], halo_far[spans[g]], halo_from_after[spans[g]])

    for landed in waits:
        landed()

    def collect(part, carry):
        rows = pl.ds(pl.multiple_of(part * CHUNK * EDGE, CHUNK * EDGE), CHUNK * EDGE)
        block = iota((1, depth), 1) // EDGE
        totals = []
        for half in range(CUBE // depth):
            total = None
            for n in range(per_half):
                f = half * per_half + n
                box = ext[pl.ds(starts[at_x, f] + part * CHUNK, CHUNK), pl.ds(starts[at_y, f], EDGE), :]
                box = pltpu.roll(box.reshape(CHUNK * EDGE, depth), starts[turn_from, f], 1)
                total = box if n == 0 else jnp.where(block == n, box, total)
            totals.append(total)
        high, low = split(jnp.concatenate(totals, axis=1) * psi[rows, :])
        value = dot(high, taps[0]) + (dot(high, taps[1]) + dot(low, taps[0]))
        high, low = split(jnp.where(iota((1, CUBE), 1) < live[0] * EDGE, value, 0.0))
        boxes[0, rows, :] = high
        boxes[1, rows, :] = low
        return carry

    lax.fori_loop(0, EDGE // CHUNK, collect, 0, unroll=4)
    for there, descriptor in issued:
        @pl.when(there)
        def _(descriptor=descriptor):
            descriptor.wait_send()


def deliver(boxes, back, ext, hpsi_hbm, pot_hbm, hpsi, sems):
    slots, _, _ = hpsi_hbm.shape
    rows_x, rows_y, _ = pot_hbm.shape
    pot_out = pltpu.make_async_copy(ext.at[pl.ds(0, rows_x), pl.ds(0, rows_y)], pot_hbm, sems.at[0])
    pot_out.start()
    outs = [pot_out]
    for half in range(2):
        lanes, part = slice(half * 128, (half + 1) * 128), pl.ds(half * slots // 2, slots // 2)
        high, low = boxes[0, :, lanes], boxes[1, :, lanes]
        result = dot(back[0], high) + (dot(back[0], low) + dot(back[1], high))
        hpsi[part] = swap_half(result).astype(BF16).reshape(slots // 2, EDGE, CUBE)
        out = pltpu.make_async_copy(hpsi.at[part], hpsi_hbm.at[part], sems.at[1 + half])
        out.start()
        outs.append(out)
    for out in outs:
        out.wait()


def shards(n_gx, n_yz, coeffs, occupation, box_offset, live_count, synthesis, v_ext, core_density):
    slots = coeffs.shape[0]
    rows_x, rows_y, depth = v_ext.shape
    wide_x, wide_y = rows_x + EDGE, rows_y + EDGE
    exchanges = 5 + 12 * (REACH // GROUP)
    vmem = pl.BlockSpec(memory_space=pltpu.VMEM)
    hbm = pl.BlockSpec(memory_space=pltpu.HBM)
    inputs = (occupation, box_offset.T, live_count, synthesis, coeffs, v_ext, core_density)
    boxes, back, ext = pl.pallas_call(
        functools.partial(kernel, (slots, rows_x, rows_y, depth, n_gx, n_yz)),
        out_shape=(
            pltpu.VMEM((2, CUBE, CUBE), BF16),
            pltpu.VMEM((2, CUBE, CUBE), BF16),
            pltpu.VMEM((wide_x, wide_y, depth), F32),
        ),
        in_specs=[hbm, hbm, pl.BlockSpec(memory_space=pltpu.SMEM), hbm, hbm, hbm, hbm],
        out_specs=(vmem, vmem, vmem),
        scratch_shapes=[
            pltpu.SMEM(occupation.shape, F32),
            pltpu.VMEM((3, slots), jnp.int32),
            pltpu.VMEM(synthesis.shape, F32),
            pltpu.VMEM(coeffs.shape, BF16),
            pltpu.VMEM(v_ext.shape, F32),
            pltpu.VMEM(v_ext.shape, F32),
            pltpu.VMEM((wide_x + 8, 128), jnp.int32),
            pltpu.SMEM((wide_x + 8, 128), jnp.int32),
            *[pltpu.VMEM((2, CUBE, CUBE), BF16)] * 3,
            *[pltpu.VMEM((CUBE, CUBE), F32)] * 2,
            pltpu.VMEM((slots, wide_y * (EDGE + 2) + rows_y, depth), F32),
            pltpu.VMEM((wide_x, wide_y, depth), F32),
            pltpu.VMEM((REACH, wide_y, depth), F32),
            pltpu.VMEM((rows_x, EDGE, depth), F32),
            pltpu.VMEM((REACH, EDGE, depth), F32),
            pltpu.VMEM((REACH, EDGE, depth), F32),
            pltpu.VMEM((REACH, wide_y, depth), F32),
            *[pltpu.VMEM((REACH, EDGE, depth), F32)] * 8,
            pltpu.SemaphoreType.DMA((len(inputs) - 1,)),
            pltpu.SemaphoreType.DMA,
            pltpu.SemaphoreType.DMA((exchanges,)),
            pltpu.SemaphoreType.DMA((exchanges,)),
        ],
        compiler_params=pltpu.CompilerParams(
            collective_id=0, has_side_effects=True, vmem_limit_bytes=40 * 1024 * 1024
        ),
    )(*(v if v is live_count else pltpu.with_memory_space_constraint(v, pltpu.HBM) for v in inputs))
    return pl.pallas_call(
        deliver,
        out_shape=(jax.ShapeDtypeStruct(coeffs.shape, BF16), jax.ShapeDtypeStruct(v_ext.shape, F32)),
        in_specs=[vmem, vmem, vmem],
        out_specs=(hbm, hbm),
        scratch_shapes=[pltpu.VMEM(coeffs.shape, BF16), pltpu.SemaphoreType.DMA((3,))],
        compiler_params=pltpu.CompilerParams(vmem_limit_bytes=16 * 1024 * 1024),
    )(boxes, back, ext)


def solution(mesh):
    placed = (
        P(("gx", "yz"), None, None),
        P(("gx", "yz")),
        P(("gx", "yz"), None),
        P(("gx", "yz")),
        P(),
        P("gx", "yz", None),
        P("gx", "yz", None),
    )
    return jax.shard_map(
        functools.partial(shards, mesh.shape["gx"], mesh.shape["yz"]),
        mesh=mesh,
        in_specs=placed,
        out_specs=(P(("gx", "yz"), None, None), P("gx", "yz", None)),
        check_vma=False,
    )
```

```python
import functools

import jax
import jax.numpy as jnp
from jax import lax
from jax.experimental import pallas as pl
from jax.experimental.pallas import tpu as pltpu
from jax.sharding import PartitionSpec as P

XC_COEF = -0.9847450218426964
EDGE = 16
CUBE = EDGE * EDGE
REACH = EDGE - 1
CHUNK = 4
GROUP = 5
F32 = jnp.float32
BF16 = jnp.bfloat16
HIGHEST = lax.Precision.HIGHEST
MESH = pl.DeviceIdType.MESH


def iota(shape, dim):
    return lax.broadcasted_iota(jnp.int32, shape, dim)


def split(value):
    high = value.astype(BF16)
    low = (value - high.astype(F32)).astype(BF16)
    return high, low


def dot(left, right):
    return lax.dot_general(left, right, (((1,), (0,)), ((), ())), preferred_element_type=F32)


def swap_blocks(value):
    half = EDGE // 2
    tiles = [
        [[value[p * EDGE : (p + 1) * EDGE, t * 128 : (t + 1) * 128] for p in range(u * half, (u + 1) * half)] for t in range(2)]
        for u in range(2)
    ]
    block = iota((EDGE, 128), 1) // EDGE
    rows = []
    for u in range(2):
        parts = []
        for t in range(2):
            part = tiles[t][u]
            for step in (1, 2, 4):
                there = (block & step) != 0
                part = [
                    jnp.where(there, part[p], pltpu.roll(part[p - step], 128 - step * EDGE, 1))
                    if p & step
                    else jnp.where(there, pltpu.roll(part[p + step], step * EDGE, 1), part[p])
                    for p in range(half)
                ]
            parts.append(jnp.concatenate(part, axis=0))
        rows.append(jnp.concatenate(parts, axis=1))
    return jnp.concatenate(rows, axis=0)


def kernel(
    sizes,
    occ_hbm, off_hbm, live, syn_hbm, coef_hbm, vext_hbm, core_hbm,
    boxes, back, ext,
    occ, off_rows, syn_ref, coef, vext, core, start_rows, starts,
    kron, filt, taps, psi, square, padded, partial, from_x, from_y, from_after, vext_far,
    from_next, vext_next, vext_corner, side_far, side_edge, halo_far, halo_edge, halo_from_y, halo_from_after,
    in_sems, table_sem, send_sems, recv_sems,
):
    slots, rows_x, rows_y, depth, n_gx, n_yz = sizes
    gx, yz = lax.axis_index("gx"), lax.axis_index("yz")
    wide_y = rows_y + EDGE
    stride = wide_y
    per_half = depth // EDGE

    inputs = (
        (coef_hbm, coef), (off_hbm, off_rows), (syn_hbm, syn_ref), (occ_hbm, occ),
        (core_hbm, core), (vext_hbm, vext),
    )
    loads = [pltpu.make_async_copy(src, dst, in_sems.at[n]) for n, (src, dst) in enumerate(inputs)]
    for load in loads:
        load.start()
    load_coef, load_off_rows, load_syn, load_occ, load_core, load_vext = loads

    after_x, before_x = gx < n_gx - 1, gx > 0
    after_y, before_y = yz < n_yz - 1, yz > 0
    next_x, next_y, last_x, last_y = (gx + 1, yz), (gx, yz + 1), (gx - 1, yz), (gx, yz - 1)
    odd = lax.rem(gx, 2) == 1
    even = jnp.logical_not(odd)
    alone, feeds, takes = odd & after_x, even & before_x, even & after_x
    barrier = pltpu.get_barrier_semaphore()
    neighbours = 0
    for there, device in ((after_x, next_x), (after_y, next_y), (before_x, last_x), (before_y, last_y)):
        @pl.when(there)
        def _(device=device):
            pl.semaphore_signal(barrier, inc=1, device_id=device, device_id_type=MESH)

        neighbours = neighbours + there.astype(jnp.int32)

    for ref in (from_y, halo_from_y):
        ref[:, REACH:, :] = jnp.zeros((ref.shape[0], EDGE - REACH, depth), F32)

    @pl.when(jnp.logical_not(before_x))
    def _():
        from_x[...] = jnp.zeros_like(from_x)

    @pl.when(jnp.logical_not(before_y))
    def _():
        from_y[...] = jnp.zeros_like(from_y)
        halo_from_y[...] = jnp.zeros_like(halo_from_y)

    @pl.when(jnp.logical_not(after_y))
    def _():
        for ref in (from_after, halo_from_after, vext_far, vext_corner):
            ref[...] = jnp.zeros_like(ref)

    def clear(slot, carry):
        for plane in range(EDGE + 3):
            padded[slot, pl.ds(stride * plane, rows_y), :] = jnp.zeros((rows_y, depth), F32)
        for plane in (0, EDGE + 1):
            padded[slot, pl.ds(stride * plane + rows_y, EDGE), :] = jnp.zeros((EDGE, depth), F32)
        return carry

    lax.fori_loop(0, slots, clear, 0)

    at_x, at_y, at_z, turn_to, turn_from = (rows_x + EDGE + n for n in range(5))
    load_off_rows.wait()
    begin_x = jnp.clip(off_rows[0:1, :] - gx * rows_x, 0, rows_x - 1)
    begin_y = jnp.clip(off_rows[1:2, :] - yz * rows_y, 0, rows_y - 1)
    plane = jnp.clip(iota((rows_x + EDGE, slots), 0) - begin_x + 1, 0, EDGE + 1)
    begin_z = off_rows[2:3, :]
    turn = begin_z - (iota((1, slots), 1) % per_half) * EDGE
    start_rows[: rows_x + EDGE, :slots] = plane * stride + rows_y - begin_y
    for n, value in enumerate((begin_x, begin_y, begin_z, turn & (depth - 1), (-turn) & (depth - 1))):
        start_rows[rows_x + EDGE + n : rows_x + EDGE + n + 1, :slots] = value
    table = pltpu.make_async_copy(start_rows, starts, table_sem)
    table.start()

    load_syn.wait()
    syn = syn_ref[...]
    lane = iota((EDGE, CUBE), 1)
    row = iota((EDGE, CUBE), 0)
    inside, outside = (lane % EDGE == row).astype(F32), (lane // EDGE == row).astype(F32)

    def exact(contract, right):
        return lax.dot_general(
            syn, right, (((contract,), (0,)), ((), ())), precision=HIGHEST, preferred_element_type=F32)

    by_i, by_j, by_a, by_b = exact(1, inside), exact(1, outside), exact(0, outside), exact(0, inside)
    for n in range(EDGE):
        rows = slice(n * EDGE, (n + 1) * EDGE)
        here = lane // EDGE == n
        for refs, value in (
            (kron, by_i[n : n + 1, :] * by_j),
            (back, by_b[n : n + 1, :] * by_a),
            (filt, jnp.where(here, by_b, 0.0)),
            (taps, jnp.where(here, by_i, 0.0)),
        ):
            high, low = split(value)
            refs[0, rows, :] = high
            refs[1, rows, :] = low

    load_occ.wait()
    load_coef.wait()
    swapped = swap_blocks(coef[...].reshape(slots * EDGE, CUBE).astype(F32)).astype(BF16)
    inner_high, inner_low = split(dot(kron[0], swapped) + dot(kron[1], swapped))
    psi[...] = dot(inner_high, filt[0]) + (dot(inner_low, filt[0]) + dot(inner_high, filt[1]))

    owner = iota((1, CUBE), 1) // EDGE
    weights = jnp.zeros((1, CUBE), F32)
    for f in range(slots):
        weights = jnp.where(owner == f, jnp.where(f < live[0], occ[f], 0.0), weights)
    square[...] = psi[...] * psi[...] * weights

    def place(n, carry):
        for half in range(CUBE // depth):
            f = half * per_half + n
            value = pltpu.roll(square[:, half * depth : (half + 1) * depth], starts[turn_to, f], 1)
            along = iota((1, depth), 1) - starts[at_z, f]
            value = jnp.where((along >= 0) & (along < EDGE), value, 0.0)
            for a in range(EDGE):
                padded[f, pl.ds(stride * (a + 1) + rows_y, EDGE), :] = value[a * EDGE : (a + 1) * EDGE, :]
        return carry

    issued = []

    def copy(there, src, dst, device, arrives):
        index = len(issued)
        descriptor = pltpu.make_async_remote_copy(
            src_ref=src, dst_ref=dst, send_sem=send_sems.at[index], recv_sem=recv_sems.at[index],
            device_id=device, device_id_type=MESH,
        )

        @pl.when(there)
        def _():
            descriptor.start()

        issued.append((there, descriptor))

        def landed():
            @pl.when(arrives)
            def _():
                descriptor.wait_recv()

        return landed

    groups = REACH // GROUP
    rest = rows_x - REACH
    edge, inner, far = pl.ds(0, EDGE), pl.ds(EDGE, rows_y - EDGE), pl.ds(rows_y, EDGE)
    edge_sent, far_sent = pl.ds(0, REACH), pl.ds(rows_y, REACH)
    spans = [pl.ds(g * GROUP, GROUP) for g in range(groups)]
    beyond = [pl.ds(rows_x + g * GROUP, GROUP) for g in range(groups)]
    others = pl.ds(REACH, rest)

    pl.semaphore_wait(barrier, neighbours)
    load_vext.wait()
    first = pl.ds(0, REACH)
    vext_in = copy(before_y, vext.at[first, edge_sent], vext_far.at[:, edge_sent], last_y, after_y)

    table.wait()
    lax.fori_loop(0, per_half, place, 0, unroll=4)

    def sum_planes(first, count, unit, own):
        def body(step, carry):
            x = first + step * unit
            totals = [None] * unit
            for f in range(slots):
                for n in range(unit):
                    rows = padded[f, pl.ds(starts[x + n, f], wide_y), :]
                    totals[n] = rows if f == 0 else totals[n] + rows
            for n in range(unit):
                if own:
                    partial[x + n, :rows_y, :] = totals[n][:rows_y] + core[x + n]
                    partial[x + n, rows_y:, :] = totals[n][rows_y:]
                else:
                    partial[x + n] = totals[n]
            return carry

        lax.fori_loop(0, count // unit, body, 0)

    load_core.wait()
    far_in, edge_in, inner_in, next_in = [], [], [], []
    for g in range(groups):
        sum_planes(g * GROUP, GROUP, GROUP, True)
        for rows in (far_sent, edge):
            next_in.append(copy(feeds, partial.at[spans[g], rows], from_next.at[spans[g], rows], last_x, alone))
        if g == 0:
            sum_planes(REACH, rest, 3, True)
            rest_in = copy(after_y, partial.at[others, far_sent], from_y.at[others, edge_sent], next_y, before_y)
        sum_planes(rows_x + g * GROUP, GROUP, GROUP, False)
        far_in.append(copy(
            after_x, partial.at[beyond[g], far_sent], from_x.at[spans[g], far_sent], next_x, before_x))
        edge_in.append(copy(after_x, partial.at[beyond[g], edge], from_x.at[spans[g], edge], next_x, before_x))

    vext_next_in = copy(feeds, vext.at[first, edge], vext_next, last_x, alone)

    onward_in, back_in, halo_onward_in, halo_back_in = [], [], [], []
    for g in range(groups):
        far_in[g]()
        side_far[spans[g]] = partial[spans[g], far, :] + from_x[spans[g], far, :]
        onward_in.append(copy(after_y, side_far.at[spans[g], edge_sent], from_y.at[spans[g], edge_sent], next_y, before_y))
        edge_in[g]()
        side_edge[spans[g]] = partial[spans[g], edge, :] + from_x[spans[g], edge, :]
        back_in.append(copy(before_y, side_edge.at[spans[g], edge_sent], from_after.at[spans[g], edge_sent], last_y, after_y))
    for g in range(groups):
        inner_in.append(copy(after_x, partial.at[beyond[g], inner], from_x.at[spans[g], inner], next_x, before_x))
    vext_in()
    vext_corner_in = copy(feeds & after_y, vext_far.at[:, edge_sent], vext_corner.at[:, edge_sent], last_x, alone & after_y)
    def potential(planes, rows, external, *densities):
        density = functools.reduce(jnp.add, densities)
        ext[planes, rows, :] = external + XC_COEF * jnp.exp2(jnp.log2(density) * (1.0 / 3.0))

    waits = []
    rest_in()
    potential(others, edge, vext[others, edge, :], partial[others, edge, :], from_y[others])
    waits.append(copy(before_y, ext.at[others, edge_sent], ext.at[others, far_sent], last_y, after_y))
    for g in range(groups):
        inner_in[g]()
        potential(spans[g], inner, vext[spans[g], inner, :], partial[spans[g], inner, :], from_x[spans[g], inner, :])
        waits.append(copy(before_x, ext.at[spans[g], inner], ext.at[beyond[g], inner], last_x, after_x))
    potential(others, inner, vext[others, inner, :], partial[others, inner, :])
    for g in range(groups):
        next_in[2 * g]()
        next_in[2 * g + 1]()

        @pl.when(alone)
        def _(g=g):
            halo_far[spans[g]] = partial[beyond[g], far, :] + from_next[spans[g], far, :]
            halo_edge[spans[g]] = partial[beyond[g], edge, :] + from_next[spans[g], edge, :]

        halo_onward_in.append(copy(
            alone & after_y, halo_far.at[spans[g], edge_sent], halo_from_y.at[spans[g], edge_sent], next_y, alone & before_y))
        halo_back_in.append(copy(
            alone & before_y, halo_edge.at[spans[g], edge_sent], halo_from_after.at[spans[g], edge_sent], last_y, alone & after_y))
        onward_in[g]()
        potential(spans[g], edge, vext[spans[g], edge, :], side_edge[spans[g]], from_y[spans[g]])
        waits.append(copy(odd, ext.at[spans[g], edge], ext.at[beyond[g], edge], last_x, takes))
        back_in[g]()
        potential(spans[g], far, vext_far[spans[g]], side_far[spans[g]], from_after[spans[g]])
        waits.append(copy(odd, ext.at[spans[g], far_sent], ext.at[beyond[g], far_sent], last_x, takes))
    vext_next_in()
    vext_corner_in()
    for g in range(groups):
        halo_onward_in[g]()
        halo_back_in[g]()

        @pl.when(alone)
        def _(g=g):
            potential(beyond[g], edge, vext_next[spans[g]], halo_edge[spans[g]], halo_from_y[spans[g]])
            potential(beyond[g], far, vext_corner[spans[g]], halo_far[spans[g]], halo_from_after[spans[g]])

    for landed in waits:
        landed()

    def collect(part, carry):
        rows = pl.ds(pl.multiple_of(part * CHUNK * EDGE, CHUNK * EDGE), CHUNK * EDGE)
        block = iota((1, depth), 1) // EDGE
        totals = []
        for half in range(CUBE // depth):
            total = None
            for n in range(per_half):
                f = half * per_half + n
                box = ext[pl.ds(starts[at_x, f] + part * CHUNK, CHUNK), pl.ds(starts[at_y, f], EDGE), :]
                box = pltpu.roll(box.reshape(CHUNK * EDGE, depth), starts[turn_from, f], 1)
                total = box if n == 0 else jnp.where(block == n, box, total)
            totals.append(total)
        high, low = split(jnp.concatenate(totals, axis=1) * psi[rows, :])
        value = dot(high, taps[0]) + (dot(high, taps[1]) + dot(low, taps[0]))
        high, low = split(jnp.where(iota((1, CUBE), 1) < live[0] * EDGE, value, 0.0))
        boxes[0, rows, :] = high
        boxes[1, rows, :] = low
        return carry

    lax.fori_loop(0, EDGE // CHUNK, collect, 0, unroll=4)
    for there, descriptor in issued:
        @pl.when(there)
        def _(descriptor=descriptor):
            descriptor.wait_send()


def deliver(boxes, back, ext, hpsi_hbm, pot_hbm, hpsi, sems):
    slots, _, _ = hpsi_hbm.shape
    rows_x, rows_y, _ = pot_hbm.shape
    pot_out = pltpu.make_async_copy(ext.at[pl.ds(0, rows_x), pl.ds(0, rows_y)], pot_hbm, sems.at[0])
    pot_out.start()
    high, low = boxes[0], boxes[1]
    result = dot(back[0], high) + (dot(back[0], low) + dot(back[1], high))
    hpsi[...] = swap_blocks(result).astype(BF16).reshape(slots, EDGE, CUBE)
    hpsi_out = pltpu.make_async_copy(hpsi, hpsi_hbm, sems.at[1])
    hpsi_out.start()
    pot_out.wait()
    hpsi_out.wait()


def shards(n_gx, n_yz, coeffs, occupation, box_offset, live_count, synthesis, v_ext, core_density):
    slots = coeffs.shape[0]
    rows_x, rows_y, depth = v_ext.shape
    wide_x, wide_y = rows_x + EDGE, rows_y + EDGE
    exchanges = 5 + 12 * (REACH // GROUP)
    vmem = pl.BlockSpec(memory_space=pltpu.VMEM)
    hbm = pl.BlockSpec(memory_space=pltpu.HBM)
    inputs = (occupation, box_offset.T, live_count, synthesis, coeffs, v_ext, core_density)
    boxes, back, ext = pl.pallas_call(
        functools.partial(kernel, (slots, rows_x, rows_y, depth, n_gx, n_yz)),
        out_shape=(
            pltpu.VMEM((2, CUBE, CUBE), BF16),
            pltpu.VMEM((2, CUBE, CUBE), BF16),
            pltpu.VMEM((wide_x, wide_y, depth), F32),
        ),
        in_specs=[hbm, hbm, pl.BlockSpec(memory_space=pltpu.SMEM), hbm, hbm, hbm, hbm],
        out_specs=(vmem, vmem, vmem),
        scratch_shapes=[
            pltpu.SMEM(occupation.shape, F32),
            pltpu.VMEM((3, slots), jnp.int32),
            pltpu.VMEM(synthesis.shape, F32),
            pltpu.VMEM(coeffs.shape, BF16),
            pltpu.VMEM(v_ext.shape, F32),
            pltpu.VMEM(v_ext.shape, F32),
            pltpu.VMEM((wide_x + 8, 128), jnp.int32),
            pltpu.SMEM((wide_x + 8, 128), jnp.int32),
            *[pltpu.VMEM((2, CUBE, CUBE), BF16)] * 3,
            *[pltpu.VMEM((CUBE, CUBE), F32)] * 2,
            pltpu.VMEM((slots, wide_y * (EDGE + 2) + rows_y, depth), F32),
            pltpu.VMEM((wide_x, wide_y, depth), F32),
            pltpu.VMEM((REACH, wide_y, depth), F32),
            pltpu.VMEM((rows_x, EDGE, depth), F32),
            pltpu.VMEM((REACH, EDGE, depth), F32),
            pltpu.VMEM((REACH, EDGE, depth), F32),
            pltpu.VMEM((REACH, wide_y, depth), F32),
            *[pltpu.VMEM((REACH, EDGE, depth), F32)] * 8,
            pltpu.SemaphoreType.DMA((len(inputs) - 1,)),
            pltpu.SemaphoreType.DMA,
            pltpu.SemaphoreType.DMA((exchanges,)),
            pltpu.SemaphoreType.DMA((exchanges,)),
        ],
        compiler_params=pltpu.CompilerParams(
            collective_id=0, has_side_effects=True, vmem_limit_bytes=40 * 1024 * 1024
        ),
    )(*(v if v is live_count else pltpu.with_memory_space_constraint(v, pltpu.HBM) for v in inputs))
    return pl.pallas_call(
        deliver,
        out_shape=(jax.ShapeDtypeStruct(coeffs.shape, BF16), jax.ShapeDtypeStruct(v_ext.shape, F32)),
        in_specs=[vmem, vmem, vmem],
        out_specs=(hbm, hbm),
        scratch_shapes=[pltpu.VMEM(coeffs.shape, BF16), pltpu.SemaphoreType.DMA((2,))],
        compiler_params=pltpu.CompilerParams(vmem_limit_bytes=16 * 1024 * 1024),
    )(boxes, back, ext)


def solution(mesh):
    placed = (
        P(("gx", "yz"), None, None),
        P(("gx", "yz")),
        P(("gx", "yz"), None),
        P(("gx", "yz")),
        P(),
        P("gx", "yz", None),
        P("gx", "yz", None),
    )
    return jax.shard_map(
        functools.partial(shards, mesh.shape["gx"], mesh.shape["yz"]),
        mesh=mesh,
        in_specs=placed,
        out_specs=(P(("gx", "yz"), None, None), P("gx", "yz", None)),
        check_vma=False,
    )
```
